512 devices in a mesh: dp: 32 (over x_lo, y, core), mp: 16 (over x_hi, z).
Axes of the slice: x: 4 (x_hi: 2, x_lo: 2; x = x_hi * 2 + x_lo), y: 8, z: 8, core: 2. Of those that a mesh axis runs over, the one named last changes fastest.
Arguments:
- layer_input: bfloat16 [512, 2, 8192], P('dp', None, 'mp'), may hold values from -90 to 90
- input_norm_gain: bfloat16 [8192], P('mp'), may hold values from 0.25 to 1.75
- key_matrix: bfloat16 [8192, 1024], P('mp'), may hold values from -0.09375 to 0.09375
- value_matrix: bfloat16 [8192, 1024], P('mp'), may hold values from -0.09375 to 0.09375
- adapter_down_factors: bfloat16 [2048, 16, 8192], P('dp', None, 'mp'), may hold values from -0.0625 to 0.0625
- adapter_up_factors: bfloat16 [2048, 16, 1024], P('dp', None, 'mp'), may hold values from -0.75 to 0.75
- adapter_storage_spot: int32 [2048], replicated, may hold values from 0 to 2047, as said below
- flight_adapter_ids: int32 [64], replicated, may hold values from 0 to 2047, as said below
- row_adapter_slot: int32 [512, 1], P('dp'), may hold values from 0 to 63
- lengths: int32 [512], P('dp'), may hold values from 2 to 384, as said below
- queries: bfloat16 [512, 2, 16, 512], P('dp', None, 'mp'), may hold values from -5 to 5
- key_value_cache: bfloat16 [512, 16, 384, 128], P('dp', 'mp'), may hold values from -5 to 5
Outputs:
- context: bfloat16 [512, 2, 16, 512], P('dp', None, 'mp')
- newest_cache_entries: bfloat16 [512, 2, 16, 128], P('dp', None, 'mp')
The draws below stay inside these ranges and needn't reach their ends.
Inputs may be any that keep to these rules, and one draw needn't show every extreme that they name: `adapter_storage_spot`: A permutation. Storage positions g * 64 to (g + 1) * 64 - 1 are those of adapter_down_factors and adapter_up_factors on index g of dp. Distinct ids. The storage positions adapter_storage_spot[flight_adapter_ids] fall at most 4 times into one block of 64 positions, and exactly 4 times into some block. `lengths`: some row has exactly 384.
All inputs are finite; a program needn't handle non-finite values.
Results may differ from the reference program's by a relative error of at most 0.0054.
Values may be sent and summed in bfloat16 or wider, within the bound.
A program may use at most 64 MiB of HBM per device.

```python
import math
import jax
import jax.numpy as jnp
from jax import lax

MODEL_WIDTH = 8192
KEY_HEADS = 8
QUERY_PER_KEY = 8
HEAD_SIZE = 128
HALF_HEAD = 64
ADAPTER_RANK = 16
ADP_GRP = 64
CAP = 4
CACHE_SLOTS = 384
DECODE_STEPS = 2
ROW_TOTAL = 512
ACTIVE = 64
ADAPTER_COUNT = 2048


def pool_plan(key):
    group_total = ADAPTER_COUNT // ADP_GRP
    home_map = jax.random.permutation(jax.random.fold_in(key, 101), ADAPTER_COUNT).astype(jnp.int32)
    first_share = jax.random.randint(jax.random.fold_in(key, 102), (group_total // 2,), 0, CAP + 1)
    first_share = first_share.at[0].set(CAP)
    counts = jnp.stack([first_share, CAP - first_share], axis=1).reshape(group_total)
    counts = jax.random.permutation(jax.random.fold_in(key, 103), counts)
    raw_scores = jax.random.randint(jax.random.fold_in(key, 104), (group_total, ADP_GRP), 0, 2 ** 20)
    distinct = raw_scores * ADP_GRP + jnp.arange(ADP_GRP, dtype=jnp.int32)[None, :]
    order = jnp.argsort(distinct, axis=1, stable=True)[:, :CAP].astype(jnp.int32)
    storage = jnp.arange(group_total, dtype=jnp.int32)[:, None] * ADP_GRP + order
    used = (jnp.arange(CAP, dtype=jnp.int32)[None, :] < counts[:, None]).astype(jnp.int32)
    ranking = jnp.argsort(1 - used.reshape(-1), stable=True)
    chosen = storage.reshape(-1)[ranking[:ACTIVE]]
    chosen = jax.random.permutation(jax.random.fold_in(key, 106), chosen)
    inverse = jnp.argsort(home_map, stable=True).astype(jnp.int32)
    return (home_map, inverse[chosen].astype(jnp.int32))


def draw_adapter_storage_spot(key, part):
    home_map, chosen_ids = pool_plan(key)
    return home_map


def draw_flight_adapter_ids(key, part):
    home_map, chosen_ids = pool_plan(key)
    return chosen_ids


def draw_lengths(key, part):
    key = jax.random.fold_in(key, 7)
    value_rows = jax.random.randint(jax.random.fold_in(key, 1), (ROW_TOTAL,), 2, CACHE_SLOTS + 1)
    filled = jax.random.randint(jax.random.fold_in(key, 2), (), 0, ROW_TOTAL)
    return value_rows.at[filled].set(CACHE_SLOTS).astype(jnp.int32)


def draw_layer_input(key, part):
    key = jax.random.fold_in(key, 11)
    row_scale = jnp.exp(jax.random.uniform(jax.random.fold_in(key, 1), (ROW_TOTAL, DECODE_STEPS, 1), jnp.float32, math.log(0.5), math.log(5.0)))
    column_ramp = jnp.exp(jnp.arange(MODEL_WIDTH, dtype=jnp.float32) / MODEL_WIDTH * math.log(3.0))
    column_rough = jnp.exp(jax.random.uniform(jax.random.fold_in(key, 2), (MODEL_WIDTH,), jnp.float32, -0.35, 0.35))
    base = jnp.clip(jax.random.normal(jax.random.fold_in(key, 3), (ROW_TOTAL, DECODE_STEPS, MODEL_WIDTH), jnp.float32), -4.0, 4.0)
    return (base * row_scale * column_ramp * column_rough).astype(jnp.bfloat16)


def draw_queries(key, part):
    key = jax.random.fold_in(key, 13)
    value_rows = jnp.clip(jax.random.normal(jax.random.fold_in(key, 1), (ROW_TOTAL, DECODE_STEPS, 2 * KEY_HEADS, QUERY_PER_KEY, HALF_HEAD), jnp.float32), -5.0, 5.0)
    return value_rows.reshape(ROW_TOTAL, DECODE_STEPS, 2 * KEY_HEADS, QUERY_PER_KEY * HALF_HEAD).astype(jnp.bfloat16)


def draw_key_value_cache(key, part):
    key = jax.random.fold_in(key, 17)
    value_rows = jnp.clip(jax.random.normal(jax.random.fold_in(key, 1), (ROW_TOTAL, 2 * KEY_HEADS, CACHE_SLOTS, HEAD_SIZE), jnp.float32), -5.0, 5.0)
    return value_rows.astype(jnp.bfloat16)


def with_spikes(result, stream_key, source, target, blocks, factor):
    def block_of(axis_at):
        return (jnp.arange(result.shape[axis_at]) // (result.shape[axis_at] // blocks)).reshape((-1,) + (1,) * (result.ndim - 1 - axis_at))

    first = jax.random.permutation(stream_key, blocks)[block_of(target)]
    second = (block_of(target) + blocks // 2) % blocks
    return jnp.where((block_of(source) == first) | (block_of(source) == second), factor * result, result)


def level_of(key, shape, split, low, largest):
    level, own = 1.0, jax.random.fold_in(key, 6)
    for axis_at, shards_of in split:
        steps = jnp.exp(jax.random.uniform(jax.random.fold_in(own, axis_at), (shards_of,), jnp.float32, low / len(split), largest / len(split)))
        level = level * jnp.repeat(steps, shape[axis_at] // shards_of).reshape([-1 if axis == axis_at else 1 for axis in range(len(shape))])
    return level


def different_ones(key, rows, amount, top, lift):
    order = jax.random.permutation(jax.random.fold_in(key, 1), amount)
    pull = order
    for power in range(3):
        pull = pull * pull // amount
    pull = pull * lift // amount
    lots = jax.random.randint(jax.random.fold_in(key, 2), (rows, amount), 0, 4096) + pull
    sure = jax.random.permutation(jax.random.fold_in(key, 3), rows)[jnp.arange(amount) % rows]
    lots = jnp.where(jnp.arange(rows)[:, None] == sure[None, :], 1 << 14, lots)
    score = lots * amount + jnp.arange(amount)
    return lax.top_k(score.astype(jnp.int32), top)[1].astype(jnp.int32)


def noise(stream_key, dims, deviation, limit, split=(), kind=jnp.bfloat16):
    values = jax.random.normal(stream_key, dims, jnp.float32) * deviation
    if len(split) > 0:
        values = level_of(stream_key, dims, split, -0.22, 0.18) * values
    return jnp.clip(values, min=-limit, max=limit).astype(kind)


def noise_with(rng, extent, scale, reach, cuts, heavy, kind=jnp.bfloat16):
    entries = scale * jax.random.normal(rng, extent, jnp.float32)
    if cuts:
        entries = entries * level_of(rng, extent, cuts, -0.22, 0.18)
    return jnp.clip(with_spikes(entries, jax.random.fold_in(rng, 3), *heavy), -reach, reach).astype(kind)


def setup_inputs(seed: int = 0) -> dict:
    seeds = jax.random.split(jax.random.key(seed), 13)
    return {
        "layer_input": draw_layer_input(jax.random.fold_in(seeds[12], 71), 0),
        "input_norm_gain": jnp.clip(1.0 + 0.15 * jax.random.normal(seeds[1], (MODEL_WIDTH,), jnp.float32), 0.25, 1.75).astype(jnp.bfloat16),
        "key_matrix": noise_with(seeds[2], (MODEL_WIDTH, KEY_HEADS * HEAD_SIZE), MODEL_WIDTH ** -0.5, 0.09375, ((0, 16),), (0, 1, 16, 2.0)),
        "value_matrix": noise_with(seeds[3], (MODEL_WIDTH, KEY_HEADS * HEAD_SIZE), MODEL_WIDTH ** -0.5, 0.09375, ((0, 16),), (0, 1, 16, 2.0)),
        "adapter_down_factors": noise(seeds[4], (ADAPTER_COUNT, ADAPTER_RANK, MODEL_WIDTH), MODEL_WIDTH ** -0.5, 0.0625, ((0, 32), (2, 16))),
        "adapter_up_factors": noise(seeds[5], (ADAPTER_COUNT, ADAPTER_RANK, KEY_HEADS * HEAD_SIZE), (4 * ADAPTER_RANK) ** -0.5, 0.75, ((0, 32), (2, 16))),
        "adapter_storage_spot": draw_adapter_storage_spot(jax.random.fold_in(seeds[12], 71), 0),
        "flight_adapter_ids": draw_flight_adapter_ids(jax.random.fold_in(seeds[12], 71), 0),
        "row_adapter_slot": different_ones(seeds[8], ROW_TOTAL, ACTIVE, 1, 256),
        "lengths": draw_lengths(jax.random.fold_in(seeds[12], 71), 0),
        "queries": draw_queries(jax.random.fold_in(seeds[12], 71), 0),
        "key_value_cache": draw_key_value_cache(jax.random.fold_in(seeds[12], 71), 0),
    }


NORM_EPSILON = 1e-05
ADAPTER_SCALE = 2.0
ROPE_LOG_BASE = math.log(500000.0)
MASKED_SCORE = -1e+30

def rotate_pieces(key_lin, lengths, half_head_index):
    half_head_width = key_lin.shape[3]
    decode_step_count = key_lin.shape[1]
    coords = half_head_index[:, None] * half_head_width + jnp.arange(half_head_width, dtype=jnp.int32)[None, :]
    pair_index = (coords // 2).astype(jnp.float32)
    frequency = jnp.exp(-(2.0 * pair_index / (2 * half_head_width)) * ROPE_LOG_BASE)
    position = (lengths[:, None] + jnp.arange(decode_step_count, dtype=jnp.int32)[None, :]).astype(jnp.float32)
    angles = position[:, :, None, None] * frequency[None, None, :, :]
    cosine = jnp.cos(angles[..., 0::2])
    sine_part = jnp.sin(angles[..., 0::2])
    even_part = key_lin[..., 0::2]
    odd_part = key_lin[..., 1::2]
    rotated = jnp.stack([even_part * cosine - odd_part * sine_part, even_part * sine_part + odd_part * cosine], axis=-1)
    return rotated.reshape(key_lin.shape)

def join_halves(pieces, half_head_width, upper):
    lower_part = pieces[:, :, 0]
    upper_part = pieces[:, :, 1]
    if upper:
        return jnp.concatenate([lower_part[..., half_head_width:], upper_part[..., half_head_width:]], axis=-1)
    return jnp.concatenate([lower_part[..., :half_head_width], upper_part[..., :half_head_width]], axis=-1)

def reference(layer_input, input_norm_gain, key_matrix, value_matrix, adapter_down_factors, adapter_up_factors, adapter_storage_spot, flight_adapter_ids, row_adapter_slot, lengths, queries, key_value_cache):
    total_rows, decode_step_count, width = layer_input.shape
    half_head_width = HEAD_SIZE // 2
    hidden = layer_input.astype(jnp.float32)
    mean_square = lax.optimization_barrier(jnp.mean(hidden * hidden, axis=-1, keepdims=True))
    normalized_input = (hidden * lax.rsqrt(mean_square + NORM_EPSILON) * input_norm_gain.astype(jnp.float32)).astype(jnp.bfloat16)
    flat = normalized_input.reshape(total_rows * decode_step_count, width)
    key_lin = jnp.dot(flat, key_matrix, preferred_element_type=jnp.float32).reshape(total_rows, decode_step_count, -1)
    value_plain = jnp.dot(flat, value_matrix, preferred_element_type=jnp.float32).reshape(total_rows, decode_step_count, -1)
    slot_position = adapter_storage_spot[flight_adapter_ids]
    row_cache_position = slot_position[row_adapter_slot[:, 0]]
    down_factor_rows = adapter_down_factors[row_cache_position].astype(jnp.float32)
    up_factor_rows = adapter_up_factors[row_cache_position].astype(jnp.float32)
    adapter_rank_size = jnp.einsum('nui,nsi->nus', normalized_input.astype(jnp.float32), down_factor_rows, precision=lax.Precision.HIGHEST)
    value_linear = value_plain + ADAPTER_SCALE * jnp.einsum('jzb,jbv->jzv', adapter_rank_size, up_factor_rows, precision=lax.Precision.HIGHEST)
    portion_count = 2 * KEY_HEADS
    half_head_index = jnp.arange(portion_count, dtype=jnp.int32) // KEY_HEADS
    key_rot = rotate_pieces(key_lin.reshape(total_rows, decode_step_count, portion_count, half_head_width), lengths, half_head_index)
    new_key = key_rot.astype(jnp.bfloat16)
    new_value = value_linear.reshape(total_rows, decode_step_count, portion_count, half_head_width).astype(jnp.bfloat16)
    newest_cache_entries = jnp.concatenate([new_key, new_value], axis=-1)
    query_divided = queries.reshape(total_rows, decode_step_count, 2, KEY_HEADS, QUERY_PER_KEY, half_head_width)
    query_full = jnp.concatenate([query_divided[:, :, 0], query_divided[:, :, 1]], axis=-1).astype(jnp.float32)
    cache_divided = key_value_cache.reshape(total_rows, 2, KEY_HEADS, CACHE_SLOTS, HEAD_SIZE)
    cache_keys = jnp.concatenate([cache_divided[:, 0, :, :, :half_head_width], cache_divided[:, 1, :, :, :half_head_width]], axis=-1).astype(jnp.float32)
    cache_values = jnp.concatenate([cache_divided[:, 0, :, :, half_head_width:], cache_divided[:, 1, :, :, half_head_width:]], axis=-1).astype(jnp.float32)
    newest_divided = newest_cache_entries.reshape(total_rows, decode_step_count, 2, KEY_HEADS, HEAD_SIZE)
    fresh_keys = join_halves(newest_divided, half_head_width, False).astype(jnp.float32)
    fresh_values = join_halves(newest_divided, half_head_width, True).astype(jnp.float32)
    scale = 1.0 / math.sqrt(HEAD_SIZE)
    score_cache = jnp.einsum('rthgd,rhcd->rthgc', query_full, cache_keys, precision=lax.Precision.HIGHEST) * scale
    valid = jnp.arange(CACHE_SLOTS, dtype=jnp.int32)[None, :] < lengths[:, None]
    score_cache = jnp.where(valid[:, None, None, None, :], score_cache, MASKED_SCORE)
    score_fresh = jnp.einsum('rthgd,rshd->rthgs', query_full, fresh_keys, precision=lax.Precision.HIGHEST) * scale
    causal = jnp.arange(decode_step_count)[None, :] <= jnp.arange(decode_step_count)[:, None]
    score_fresh = jnp.where(causal[None, :, None, None, :], score_fresh, MASKED_SCORE)
    top_score = jnp.maximum(lax.optimization_barrier(jnp.max(score_cache, axis=-1, keepdims=True)), lax.optimization_barrier(jnp.max(score_fresh, axis=-1, keepdims=True)))
    exp_cache = jnp.exp(score_cache - top_score)
    exp_fresh = jnp.exp(score_fresh - top_score)
    total = lax.optimization_barrier(jnp.sum(exp_cache, axis=-1, keepdims=True)) + lax.optimization_barrier(jnp.sum(exp_fresh, axis=-1, keepdims=True))
    weight_cache = (exp_cache / total).astype(jnp.bfloat16).astype(jnp.float32)
    weight_fresh = (exp_fresh / total).astype(jnp.bfloat16).astype(jnp.float32)
    context_full = jnp.einsum('rthgc,rhcd->rthgd', weight_cache, cache_values, precision=lax.Precision.HIGHEST)
    context_full = context_full + jnp.einsum('rthgs,rshd->rthgd', weight_fresh, fresh_values, precision=lax.Precision.HIGHEST)
    context_full = context_full.astype(jnp.bfloat16)
    context = jnp.stack([context_full[..., :half_head_width], context_full[..., half_head_width:]], axis=2)
    context = context.reshape(total_rows, decode_step_count, 2 * KEY_HEADS, QUERY_PER_KEY * half_head_width)
    return (context, newest_cache_entries)
```

```python
import math

import jax
import jax.numpy as jnp
from jax import lax
from jax.experimental import pallas as pl
from jax.experimental.pallas import tpu as pltpu
from jax.sharding import PartitionSpec as P

MESH = pl.DeviceIdType.MESH
F32 = jnp.float32
BF16 = jnp.bfloat16

NORM_EPSILON = 1e-05
ROPE_LOG_BASE = math.log(500000.0)
MASKED_SCORE = -1e30

Y, Z = 8, 8
ROWS, STEPS, CAP, RANK = 16, 2, 4, 16
TOKENS = ROWS * STEPS
GROUPS, HALF, WIDTH, SLOTS = 8, 64, 512, 384
QROWS = TOKENS * GROUPS
BLOCK = CAP * RANK

ROW_OFFS = [(k, 0, 0) for k in (0, 4, 3, 5, 2, 6, 1, 7)]
FAC_OFFS = [(0, a, b) for a in range(2) for b in range(2)]
MP_OFFS = sorted(
    [(a, b) for a in range(2) for b in range(Z) if a or b], key=lambda o: -2 * o[0] - min(o[1], Z - o[1])
)
Z_OFFS = (4, 3, 5, 2, 6, 1, 7)
NR, NF = len(ROW_OFFS), len(FAC_OFFS)
MET = NR * TOKENS

NN = (((1,), (0,)), ((), ()))
NT = (((1,), (1,)), ((), ()))
TN = (((0,), (0,)), ((), ()))


def dot(a, b, dims):
    return lax.dot_general(a, b, dims, preferred_element_type=F32)


def iota(shape, axis):
    return lax.broadcasted_iota(jnp.int32, shape, axis)


def body(
    x_hbm, gain_hbm, k_hbm, v_hbm, down_hbm, up_hbm, spot_hbm, ids_hbm, slot_hbm, len_hbm, q_hbm, cache_hbm,
    ctx_ref, new_ref,
    x_v, gain_v, k_v, v_v, down_v, up_v, spot_v, ids_v, slot_v, len_v, q_v, cache_v,
    flat, qexp, qown, qfull, rows, tags, facs, zsend, zrecv, xsend, xrecv, qother,
    own, other, ctxs, mps, mprecv, rets, retrecv,
    load_sem, rows_s, rows_r, tags_s, tags_r, facs_s, facs_r, z_s, z_r, x_s, x_r, q_s, q_r, sc_s, sc_r,
    mp_s, mp_r, ret_s, ret_r,
):
    dp, mp = lax.axis_index("dp"), lax.axis_index("mp")
    x_lo, y, core = dp // (2 * Y), (dp // 2) % Y, dp % 2
    half, z = mp // Z, mp % Z

    def along_dp(off, sign):
        to_y = (y + (Y + sign * off[0])) % Y
        return (((x_lo + off[1]) % 2) * (2 * Y) + to_y * 2 + (core + off[2]) % 2, mp)

    def along_mp(off):
        return (dp, ((half + off[0]) % 2) * Z + (z + off[1]) % Z)

    partner = (dp, (1 - half) * Z + z)

    barrier = pltpu.get_barrier_semaphore()
    greeted = [along_dp(o, 1) for o in ROW_OFFS + FAC_OFFS if o != (0, 0, 0)]
    greeted += [along_mp(o) for o in MP_OFFS]
    for device in greeted:
        pl.semaphore_signal(barrier, inc=1, device_id=device, device_id_type=MESH)

    def load(src, dst, n):
        copy = pltpu.make_async_copy(src, dst, load_sem.at[n])
        copy.start()
        return copy

    small = [
        load(x_hbm, x_v, 0), load(gain_hbm, gain_v, 1), load(spot_hbm, spot_v, 2), load(ids_hbm, ids_v, 3),
        load(slot_hbm, slot_v, 4), load(len_hbm, len_v, 5), load(q_hbm, q_v, 6),
    ]
    load_down, load_up = load(down_hbm, down_v, 7), load(up_hbm, up_v, 8)
    load_k, load_v = load(k_hbm, k_v, 9), load(v_hbm, v_v, 10)
    load_cache = load(cache_hbm, cache_v, 11)

    def send(src, dst, ss, rs, device):
        copy = pltpu.make_async_remote_copy(
            src_ref=src, dst_ref=dst, send_sem=ss, recv_sem=rs, device_id=device, device_id_type=MESH
        )
        copy.start()
        return copy

    for copy in small:
        copy.wait()

    for r in range(ROWS):
        flat[pl.ds(2 * r, 2), :] = x_v[r].astype(F32)
    hidden = flat[...]
    gained = (hidden * gain_v[...].astype(F32).reshape(1, WIDTH)).astype(BF16)
    rows[0] = gained
    square = jnp.sum(hidden * hidden, axis=1, keepdims=True)
    lane_t, sub_t = iota((TOKENS, 128), 1), iota((TOKENS, 128), 0)
    diagonal = lane_t == sub_t
    square_row = jnp.sum(jnp.where(diagonal, square, 0.0), axis=0, keepdims=True)

    sub16, lane16 = iota((ROWS, 128), 0), iota((ROWS, 128), 1)
    slot_wide = jnp.pad(slot_v[...].astype(F32), ((0, 0), (0, 128 - ROWS)))
    slot_col = jnp.sum(jnp.where(sub16 == lane16, slot_wide, 0.0), axis=1, keepdims=True)
    tag_row = jnp.sum(
        jnp.where(sub16 == (lane16 % TOKENS) // STEPS, slot_col, 0.0), axis=0, keepdims=True
    )
    tags[0] = jnp.broadcast_to(tag_row, (8, 128))

    sub64, lane64 = iota((64, 64), 0), iota((64, 64), 1)
    ids_col = jnp.sum(jnp.where(sub64 == lane64, ids_v[...].astype(F32), 0.0), axis=1, keepdims=True)
    spots = spot_v[...].astype(F32)
    lane_n = iota((64, 128), 1).astype(F32)
    found = jnp.zeros((64, 128), F32)
    for i in range(16):
        found = found + jnp.where(ids_col - (128.0 * i) == lane_n, spots[i : i + 1, :], 0.0)
    place_col = jnp.sum(found, axis=1, keepdims=True)
    place_row = jnp.sum(jnp.where(sub64 == lane64, place_col, 0.0), axis=0, keepdims=True)
    group = dp.astype(F32)
    owner_row = jnp.floor(place_row * (1.0 / 64))
    mine_row = jnp.where(owner_row == group, 1.0, 0.0)
    mine_col = jnp.where(jnp.floor(place_col * (1.0 / 64)) == group, 1.0, 0.0)
    order_row = jnp.sum(jnp.where(sub64 < lane64, mine_col, 0.0), axis=0, keepdims=True)
    sub_f = (sub64 // RANK).astype(F32)
    picks = jnp.where(order_row == sub_f, mine_row, 0.0)
    target = jnp.sum(picks * (place_row - 64.0 * owner_row), axis=1, keepdims=True) * RANK
    target = target + (iota((64, 1), 0) % RANK).astype(F32)
    tag_col = jnp.sum(picks * (lane64 + 1).astype(F32), axis=1, keepdims=True) - 1.0
    select = jnp.where(target == iota((64, 1024), 1).astype(F32), 1.0, 0.0).astype(BF16)

    load_down.wait()
    facs[0, :, 0:WIDTH] = dot(select, down_v[...].reshape(64 * RANK, WIDTH), NN).astype(BF16)
    load_up.wait()
    up_own = dot(select, up_v[...].reshape(64 * RANK, HALF), NN).astype(BF16)
    shift = jnp.where(iota((HALF, 128), 1) == iota((HALF, 128), 0) + HALF, 1.0, 0.0).astype(BF16)
    up_wide = dot(up_own, shift, NN)
    facs[0, :, WIDTH : WIDTH + 128] = jnp.where(iota((64, 128), 1) < HALF, tag_col, up_wide).astype(BF16)

    pl.semaphore_wait(barrier, len(greeted))

    row_copies, tag_copies, fac_copies = [], [], []
    for k in range(1, NR):
        to = along_dp(ROW_OFFS[k], 1)
        row_copies.append(send(rows.at[0], rows.at[k], rows_s.at[k], rows_r.at[k], to))
        tag_copies.append(send(tags.at[0], tags.at[k], tags_s.at[k], tags_r.at[k], to))
    for k in range(1, NF):
        to = along_dp(FAC_OFFS[k], 1)
        fac_copies.append(send(facs.at[0], facs.at[k], facs_s.at[k], facs_r.at[k], to))
    q_copy = send(q_v, qother, q_s.at[0], q_r.at[0], partner)

    low = lane_t < HALF
    square_rows = jnp.broadcast_to(square_row, (8, 128))
    for w, (copy, weight) in enumerate(((load_k, k_v), (load_v, v_v))):
        copy.wait()
        part = dot(gained, weight[...], NN)
        here = slice(w * 128, w * 128 + 128)
        for j in range(4):
            first = part[:, j * 128 : j * 128 + 128]
            second = part[:, 512 + j * 128 : 512 + j * 128 + 128]
            zsend[2 * j, 0:TOKENS, here] = jnp.where(low, first, pltpu.roll(second, HALF, 1))
            zsend[2 * j + 1, 0:TOKENS, here] = jnp.where(low, pltpu.roll(first, HALF, 1), second)
        for j in range(Z):
            zsend[j, TOKENS : TOKENS + 8, here] = square_rows
    z_copies = [
        send(zsend.at[(z + k) % Z], zrecv.at[k], z_s.at[k], z_r.at[k], along_mp((0, k))) for k in Z_OFFS
    ]

    def expand(ref):
        for r in range(ROWS):
            flat[pl.ds(2 * r, 2), :] = ref[r].astype(F32)
        for g in range(GROUPS):
            tile = flat[:, (g // 2) * 128 : (g // 2) * 128 + 128]
            if g % 2:
                tile = pltpu.roll(tile, HALF, 1)
            qexp[pl.ds(g, TOKENS, stride=GROUPS), :] = jnp.where(low, tile, 0.0)
        return qexp[...]

    own_query = expand(q_v)
    qown[...] = own_query.astype(BF16)
    load_cache.wait()
    score_copies = []
    for c in range(4):
        for r in range(4 * c, 4 * c + 4):
            here = pl.ds(16 * r, 16)
            own[here, :] = dot(qown[here, :], cache_v[r], NT)
        here = pl.ds(64 * c, 64)
        score_copies.append(send(own.at[here], other.at[here], sc_s.at[c], sc_r.at[c], partner))

    for copy in row_copies + tag_copies + fac_copies:
        copy.wait_recv()
    lane_r = iota((8, 128), 1)
    tag_tiles = []
    for j in range((NR + 3) // 4):
        tile = jnp.zeros((8, 128), F32)
        for k in range(4 * j, min(4 * j + 4, NR)):
            tile = jnp.where(lane_r // TOKENS == k % 4, tags[k], tile)
        tag_tiles.append(tile)
    tag_all = jnp.concatenate(tag_tiles, axis=1)[0:1, :MET]
    fac_tag = facs[:, :, WIDTH : WIDTH + 128].reshape(NF * BLOCK, 128)[:, 0:1].astype(F32)
    same = fac_tag == tag_all
    met = dot(
        facs[:, :, 0:WIDTH].reshape(NF * BLOCK, WIDTH), rows[...].reshape(MET, WIDTH), NT
    )
    rank_part = jnp.sum(jnp.where(same, met, 0.0).reshape(NF * CAP, RANK, MET), axis=0)
    mps[...] = rank_part.astype(BF16)
    mp_copies = [
        send(mps, mprecv.at[k], mp_s.at[k], mp_r.at[k], along_mp(o)) for k, o in enumerate(MP_OFFS)
    ]

    for copy in z_copies:
        copy.wait_recv()
    total = zsend[z]
    for k in range(1, Z):
        total = total + zrecv[k]
    xsend[...] = total
    x_copy = send(xsend, xrecv, x_s.at[0], x_r.at[0], partner)

    q_copy.wait_recv()
    other_query = expand(qother)
    upper = half == 1
    first = jnp.where(upper, other_query, own_query)
    second = jnp.where(upper, own_query, other_query)
    qfull[...] = (first + pltpu.roll(second, HALF, 1)).astype(BF16)

    scale = 1.0 / math.sqrt(2 * HALF)
    len_wide = jnp.pad(len_v[...].astype(F32), ((0, 0), (0, 128 - ROWS)))
    len_col = jnp.sum(
        jnp.where(iota((QROWS, 128), 1) == iota((QROWS, 128), 0) // 16, len_wide, 0.0), axis=1, keepdims=True
    )
    cache_tops, cache_sums = [], []
    for c in range(4):
        score_copies[c].wait_recv()
        here = pl.ds(64 * c, 64)
        scores = (own[here, :] + other[here, :]) * scale
        valid = iota((64, SLOTS), 1).astype(F32) < len_col[64 * c : 64 * c + 64]
        scores = jnp.where(valid, scores, MASKED_SCORE)
        top = jnp.max(scores, axis=1, keepdims=True)
        spread = jnp.exp(scores - top)
        cache_tops.append(top)
        cache_sums.append(jnp.sum(spread, axis=1, keepdims=True))
        spread = spread.astype(BF16)
        for r in range(4):
            ctxs[pl.ds(64 * c + 16 * r, 16), :] = dot(spread[16 * r : 16 * r + 16], cache_v[4 * c + r], NN)
    cache_top = jnp.concatenate(cache_tops, axis=0)
    cache_sum = jnp.concatenate(cache_sums, axis=0)

    x_copy.wait_recv()
    total = xsend[...] + xrecv[...]
    squares = jnp.sum(jnp.where(diagonal, total[TOKENS : TOKENS + 1, 0:128], 0.0), axis=1, keepdims=True)
    norm = lax.rsqrt(squares * (1.0 / (16 * WIDTH)) + NORM_EPSILON)
    key_lin = total[0:TOKENS, 0:128] * norm
    pair = (lane_t // 2).astype(F32)
    frequency = jnp.exp(-(2.0 * pair / (2 * HALF)) * ROPE_LOG_BASE)
    start = jnp.sum(jnp.where(lane_t == sub_t // STEPS, len_wide, 0.0), axis=1, keepdims=True)
    angle = (start + (sub_t % STEPS).astype(F32)) * frequency
    even = lane_t % 2 == 0
    turned = jnp.where(even, -pltpu.roll(key_lin, 127, 1), pltpu.roll(key_lin, 1, 1))
    key_rot = key_lin * jnp.cos(angle) + turned * jnp.sin(angle)
    new_key = key_rot.astype(BF16)
    fresh = dot(qfull[...], new_key, NT) * scale
    q_sub, t_lane = iota((QROWS, TOKENS), 0), iota((QROWS, TOKENS), 1)
    counts = (t_lane // STEPS == q_sub // 16) & (t_lane % STEPS <= (q_sub // GROUPS) % STEPS)
    fresh = jnp.where(counts, fresh, MASKED_SCORE)
    top = jnp.maximum(cache_top, jnp.max(fresh, axis=1, keepdims=True))
    fresh_exp = jnp.exp(fresh - top)
    shrink = jnp.exp(cache_top - top)
    inverse = 1.0 / (cache_sum * shrink + jnp.sum(fresh_exp, axis=1, keepdims=True))
    fresh_weights = (fresh_exp * inverse).astype(BF16)
    ctxs[...] = ctxs[...] * (shrink * inverse)
    key_own = jnp.where(upper, pltpu.roll(key_rot, HALF, 1), key_rot)
    value_base = total[0:TOKENS, 128:256]
    value_base = jnp.where(upper, value_base, pltpu.roll(value_base, HALF, 1))

    for copy in mp_copies:
        copy.wait_recv()
    rank = rank_part
    for k in range(15):
        rank = rank + mprecv[k].astype(F32)
    spread = jnp.broadcast_to(rank[None], (NF * CAP, RANK, MET)).reshape(NF * BLOCK, MET)
    spread = jnp.where(same, spread, 0.0)
    up_all = facs[:, :, WIDTH : WIDTH + 128].reshape(NF * BLOCK, 128)
    coarse = spread.astype(BF16)
    rest = (spread - coarse.astype(F32)).astype(BF16)
    rets[...] = (dot(coarse, up_all, TN) + dot(rest, up_all, TN)).reshape(NR, TOKENS, 128)
    ret_copies = [
        send(rets.at[k], retrecv.at[k], ret_s.at[k], ret_r.at[k], along_dp(ROW_OFFS[k], -1))
        for k in range(1, NR)
    ]
    lora = rets[0]
    for copy in ret_copies:
        copy.wait_recv()
    for k in range(1, NR):
        lora = lora + retrecv[k]

    new_value = ((value_base + 2.0 * lora) * norm).astype(BF16)
    new_ref[...] = jnp.where(low, key_own, ((value_base + 2.0 * lora) * norm)).astype(BF16)
    qexp[...] = ctxs[...] + dot(fresh_weights, new_value, NN)
    for j in range(4):
        left = qexp[pl.ds(2 * j, TOKENS, stride=GROUPS), :]
        right = qexp[pl.ds(2 * j + 1, TOKENS, stride=GROUPS), :]
        ctx_ref[:, j * 128 : j * 128 + 128] = jnp.where(low, pltpu.roll(left, HALF, 1), right).astype(BF16)

    for copy in (
        row_copies + tag_copies + fac_copies + z_copies + score_copies + mp_copies + ret_copies + [q_copy, x_copy]
    ):
        copy.wait_send()


def shards(
    layer_input, input_norm_gain, key_matrix, value_matrix, adapter_down_factors, adapter_up_factors,
    adapter_storage_spot, flight_adapter_ids, row_adapter_slot, lengths, queries, key_value_cache,
):
    dma = pltpu.SemaphoreType.DMA
    loads = [
        ((ROWS, STEPS, WIDTH), BF16), ((WIDTH,), BF16), ((WIDTH, 1024), BF16), ((WIDTH, 1024), BF16),
        ((64, RANK, WIDTH), BF16), ((64, RANK, HALF), BF16), ((16, 128), jnp.int32), ((1, 64), jnp.int32),
        ((1, ROWS), jnp.int32), ((1, ROWS), jnp.int32), ((ROWS, STEPS, WIDTH), BF16), ((ROWS, SLOTS, 128), BF16),
    ]
    work = [
        ((TOKENS, WIDTH), F32),
        ((QROWS, 128), F32),
        ((QROWS, 128), BF16),
        ((QROWS, 128), BF16),
        ((NR, TOKENS, WIDTH), BF16),
        ((NR, 8, 128), F32),
        ((NF, BLOCK, WIDTH + 128), BF16),
        ((Z, TOKENS + 8, 256), F32),
        ((Z, TOKENS + 8, 256), F32),
        ((TOKENS + 8, 256), F32),
        ((TOKENS + 8, 256), F32),
        ((ROWS, STEPS, WIDTH), BF16),
        ((QROWS, SLOTS), F32),
        ((QROWS, SLOTS), F32),
        ((QROWS, 128), F32),
        ((RANK, MET), BF16),
        ((15, RANK, MET), BF16),
        ((NR, TOKENS, 128), F32),
        ((NR, TOKENS, 128), F32),
    ]
    sems = [12, NR, NR, NR, NR, NF, NF, Z, Z, 1, 1, 1, 1, 4, 4, 15, 15, NR, NR]
    any_spec = pl.BlockSpec(memory_space=pl.ANY)
    vmem_spec = pl.BlockSpec(memory_space=pltpu.VMEM)
    context, newest = pl.pallas_call(
        body,
        out_shape=(
            jax.ShapeDtypeStruct((TOKENS, WIDTH), BF16),
            jax.ShapeDtypeStruct((TOKENS, 128), BF16),
        ),
        in_specs=[any_spec] * 12,
        out_specs=(vmem_spec, vmem_spec),
        scratch_shapes=[pltpu.VMEM(*s) for s in loads + work] + [dma((n,)) for n in sems],
        compiler_params=pltpu.CompilerParams(
            collective_id=0, has_side_effects=True, vmem_limit_bytes=40 * 2**20
        ),
    )(*(pltpu.with_memory_space_constraint(a, pltpu.HBM) for a in (
        layer_input,
        input_norm_gain,
        key_matrix,
        value_matrix,
        adapter_down_factors,
        adapter_up_factors,
        adapter_storage_spot.reshape(16, 128),
        flight_adapter_ids.reshape(1, 64),
        row_adapter_slot.reshape(1, ROWS),
        lengths.reshape(1, ROWS),
        queries.reshape(ROWS, STEPS, WIDTH),
        key_value_cache.reshape(ROWS, SLOTS, 128),
    )))
    return context.reshape(ROWS, STEPS, 1, WIDTH), newest.reshape(ROWS, STEPS, 1, 128)


def solution(mesh):
    return jax.shard_map(
        shards,
        mesh=mesh,
        in_specs=(
            P("dp", None, "mp"),
            P("mp"),
            P("mp", None),
            P("mp", None),
            P("dp", None, "mp"),
            P("dp", None, "mp"),
            P(),
            P(),
            P("dp", None),
            P("dp"),
            P("dp", None, "mp", None),
            P("dp", "mp", None, None),
        ),
        out_specs=(P("dp", None, "mp", None), P("dp", None, "mp", None)),
        check_vma=False,
    )
```

```python
import math

import jax
import jax.numpy as jnp
from jax import lax
from jax.experimental import pallas as pl
from jax.experimental.pallas import tpu as pltpu
from jax.sharding import PartitionSpec as P

MESH = pl.DeviceIdType.MESH
F32 = jnp.float32
BF16 = jnp.bfloat16

NORM_EPSILON = 1e-05
ROPE_LOG_BASE = math.log(500000.0)
MASKED_SCORE = -1e30

Y, Z = 8, 8
ROWS, STEPS, CAP, RANK = 16, 2, 4, 16
TOKENS = ROWS * STEPS
GROUPS, HALF, WIDTH, SLOTS = 8, 64, 512, 384
QROWS = TOKENS * GROUPS
BLOCK = CAP * RANK

ROW_OFFS = [(k, 0, 0) for k in (0, 4, 3, 5, 2, 6, 1, 7)]
FAC_OFFS = [(0, a, b) for a in range(2) for b in range(2)]
MP_OFFS = sorted(
    [(a, b) for a in range(2) for b in range(Z) if a or b], key=lambda o: -2 * o[0] - min(o[1], Z - o[1])
)
Z_OFFS = (4, 3, 5, 2, 6, 1, 7)
NR, NF = len(ROW_OFFS), len(FAC_OFFS)
MET = NR * TOKENS

NN = (((1,), (0,)), ((), ()))
NT = (((1,), (1,)), ((), ()))
TN = (((0,), (0,)), ((), ()))


def dot(a, b, dims):
    return lax.dot_general(a, b, dims, preferred_element_type=F32)


def iota(shape, axis):
    return lax.broadcasted_iota(jnp.int32, shape, axis)


CODE_RATE, CODE_SHIFT = 1.75, 124.0


def encode(score):
    power = jnp.exp2(jnp.abs(score) * CODE_RATE - CODE_SHIFT)
    return jnp.where(score < 0.0, -power, power).astype(BF16)


def decode(code):
    power = code.astype(F32)
    size = (jnp.log2(jnp.abs(power)) + CODE_SHIFT) * (1.0 / CODE_RATE)
    return jnp.where(power < 0.0, -size, size)


def body(
    x_hbm, gain_hbm, k_hbm, v_hbm, down_hbm, up_hbm, spot_hbm, ids_hbm, slot_hbm, len_hbm, q_hbm, cache_hbm,
    ctx_ref, new_ref,
    x_v, gain_v, k_v, v_v, down_v, up_v, spot_v, ids_v, slot_v, len_v, q_v, cache_v,
    flat, qexp, qown, qfull, rows, facs, zsend, zrecv, xsend, xrecv, qother,
    own, coded, other, ctxs, mps, mprecv, rets, retrecv,
    load_sem, rows_s, rows_r, facs_s, facs_r, z_s, z_r, x_s, x_r, q_s, q_r, sc_s, sc_r,
    mp_s, mp_r, ret_s, ret_r,
):
    dp, mp = lax.axis_index("dp"), lax.axis_index("mp")
    x_lo, y, core = dp // (2 * Y), (dp // 2) % Y, dp % 2
    half, z = mp // Z, mp % Z

    def along_dp(off, sign):
        to_y = (y + (Y + sign * off[0])) % Y
        return (((x_lo + off[1]) % 2) * (2 * Y) + to_y * 2 + (core + off[2]) % 2, mp)

    def along_mp(off):
        return (dp, ((half + off[0]) % 2) * Z + (z + off[1]) % Z)

    partner = (dp, (1 - half) * Z + z)

    barrier = pltpu.get_barrier_semaphore()
    greeted = [along_dp(o, 1) for o in ROW_OFFS + FAC_OFFS if o != (0, 0, 0)]
    greeted += [along_mp(o) for o in MP_OFFS]
    for device in greeted:
        pl.semaphore_signal(barrier, inc=1, device_id=device, device_id_type=MESH)

    def load(src, dst, n):
        copy = pltpu.make_async_copy(src, dst, load_sem.at[n])
        copy.start()
        return copy

    small = [
        load(x_hbm, x_v, 0), load(gain_hbm, gain_v, 1), load(spot_hbm, spot_v, 2), load(ids_hbm, ids_v, 3),
        load(slot_hbm, slot_v, 4), load(len_hbm, len_v, 5), load(q_hbm, q_v, 6),
    ]
    load_down, load_up = load(down_hbm, down_v, 7), load(up_hbm, up_v, 8)
    load_k, load_v = load(k_hbm, k_v, 9), load(v_hbm, v_v, 10)
    load_cache = load(cache_hbm, cache_v, 11)

    def send(src, dst, ss, rs, device):
        copy = pltpu.make_async_remote_copy(
            src_ref=src, dst_ref=dst, send_sem=ss, recv_sem=rs, device_id=device, device_id_type=MESH
        )
        copy.start()
        return copy

    for copy in small:
        copy.wait()

    for r in range(ROWS):
        flat[pl.ds(2 * r, 2), :] = x_v[r].astype(F32)
    hidden = flat[...]
    gained = (hidden * gain_v[...].astype(F32).reshape(1, WIDTH)).astype(BF16)
    for j in range(4):
        rows[0, TOKENS * j : TOKENS * j + TOKENS, :] = gained[:, 128 * j : 128 * j + 128]
    square = jnp.sum(hidden * hidden, axis=1, keepdims=True)
    lane_t, sub_t = iota((TOKENS, 128), 1), iota((TOKENS, 128), 0)
    diagonal = lane_t == sub_t
    square_row = jnp.sum(jnp.where(diagonal, square, 0.0), axis=0, keepdims=True)

    sub16, lane16 = iota((ROWS, 128), 0), iota((ROWS, 128), 1)
    slot_wide = jnp.pad(slot_v[...].astype(F32), ((0, 0), (0, 128 - ROWS)))
    slot_col = jnp.sum(jnp.where(sub16 == lane16, slot_wide, 0.0), axis=1, keepdims=True)
    tag_row = jnp.sum(
        jnp.where(sub16 == (lane16 % TOKENS) // STEPS, slot_col, 0.0), axis=0, keepdims=True
    )
    rows[0, 4 * TOKENS : 4 * TOKENS + 16, :] = jnp.broadcast_to(tag_row, (16, 128)).astype(BF16)

    pl.semaphore_wait(barrier, len(greeted))

    row_copies = [
        send(rows.at[0], rows.at[k], rows_s.at[k], rows_r.at[k], along_dp(ROW_OFFS[k], 1)) for k in range(1, NR)
    ]
    sub64, lane64 = iota((64, 64), 0), iota((64, 64), 1)
    ids_col = jnp.sum(jnp.where(sub64 == lane64, ids_v[...].astype(F32), 0.0), axis=1, keepdims=True)
    spots = spot_v[...].astype(F32)
    lane_n = iota((64, 128), 1).astype(F32)
    found = jnp.zeros((64, 128), F32)
    for i in range(16):
        found = found + jnp.where(ids_col - (128.0 * i) == lane_n, spots[i : i + 1, :], 0.0)
    place_col = jnp.sum(found, axis=1, keepdims=True)
    place_row = jnp.sum(jnp.where(sub64 == lane64, place_col, 0.0), axis=0, keepdims=True)
    group = dp.astype(F32)
    owner_row = jnp.floor(place_row * (1.0 / 64))
    mine_row = jnp.where(owner_row == group, 1.0, 0.0)
    mine_col = jnp.where(jnp.floor(place_col * (1.0 / 64)) == group, 1.0, 0.0)
    order_row = jnp.sum(jnp.where(sub64 < lane64, mine_col, 0.0), axis=0, keepdims=True)
    sub_f = (sub64 // RANK).astype(F32)
    picks = jnp.where(order_row == sub_f, mine_row, 0.0)
    target = jnp.sum(picks * (place_row - 64.0 * owner_row), axis=1, keepdims=True) * RANK
    target = target + (iota((64, 1), 0) % RANK).astype(F32)
    tag_col = jnp.sum(picks * (lane64 + 1).astype(F32), axis=1, keepdims=True) - 1.0
    select = jnp.where(target == iota((64, 1024), 1).astype(F32), 1.0, 0.0).astype(BF16)

    load_down.wait()
    facs[0, :, 0:WIDTH] = dot(select, down_v[...].reshape(64 * RANK, WIDTH), NN).astype(BF16)
    load_up.wait()
    up_own = dot(select, up_v[...].reshape(64 * RANK, HALF), NN).astype(BF16)
    shift = jnp.where(iota((HALF, 128), 1) == iota((HALF, 128), 0) + HALF, 1.0, 0.0).astype(BF16)
    up_wide = dot(up_own, shift, NN)
    facs[0, :, WIDTH : WIDTH + 128] = jnp.where(iota((64, 128), 1) < HALF, tag_col, up_wide).astype(BF16)

    fac_copies = [
        send(facs.at[0], facs.at[k], facs_s.at[k], facs_r.at[k], along_dp(FAC_OFFS[k], 1)) for k in range(1, NF)
    ]
    q_copy = send(q_v, qother, q_s.at[0], q_r.at[0], partner)

    low = lane_t < HALF
    square_rows = jnp.broadcast_to(square_row, (8, 128))
    for w, (copy, weight) in enumerate(((load_k, k_v), (load_v, v_v))):
        copy.wait()
        part = dot(gained, weight[...], NN)
        here = slice(w * 128, w * 128 + 128)
        for j in range(4):
            first = part[:, j * 128 : j * 128 + 128]
            second = part[:, 512 + j * 128 : 512 + j * 128 + 128]
            zsend[2 * j, 0:TOKENS, here] = jnp.where(low, first, pltpu.roll(second, HALF, 1))
            zsend[2 * j + 1, 0:TOKENS, here] = jnp.where(low, pltpu.roll(first, HALF, 1), second)
        for j in range(Z):
            zsend[j, TOKENS : TOKENS + 8, here] = square_rows
    z_copies = [
        send(zsend.at[(z + k) % Z], zrecv.at[k], z_s.at[k], z_r.at[k], along_mp((0, k))) for k in Z_OFFS
    ]

    def expand(ref):
        for r in range(ROWS):
            flat[pl.ds(2 * r, 2), :] = ref[r].astype(F32)
        for g in range(GROUPS):
            tile = flat[:, (g // 2) * 128 : (g // 2) * 128 + 128]
            if g % 2:
                tile = pltpu.roll(tile, HALF, 1)
            qexp[pl.ds(g, TOKENS, stride=GROUPS), :] = jnp.where(low, tile, 0.0)
        return qexp[...]

    scale = 1.0 / math.sqrt(2 * HALF)
    own_query = expand(q_v)
    qown[...] = own_query.astype(BF16)
    load_cache.wait()
    for r in range(ROWS):
        here = pl.ds(16 * r, 16)
        piece = dot(qown[here, :], cache_v[r], NT) * scale
        own[here, :] = piece
        coded[here, :] = encode(piece)

    for copy in row_copies + fac_copies:
        copy.wait_recv()
    lane_r = iota((16, 128), 1)
    tag_tiles = []
    for j in range((NR + 3) // 4):
        tile = jnp.zeros((16, 128), F32)
        for k in range(4 * j, min(4 * j + 4, NR)):
            tile = jnp.where(lane_r // TOKENS == k % 4, rows[k, 4 * TOKENS : 4 * TOKENS + 16, :].astype(F32), tile)
        tag_tiles.append(tile)
    tag_all = jnp.concatenate(tag_tiles, axis=1)[0:1, :MET]
    fac_tag = facs[:, :, WIDTH : WIDTH + 128].reshape(NF * BLOCK, 128)[:, 0:1].astype(F32)
    same = fac_tag == tag_all
    features = jnp.concatenate(
        [rows[:, TOKENS * j : TOKENS * j + TOKENS, :].reshape(MET, 128) for j in range(4)], axis=1
    )
    met = dot(facs[:, :, 0:WIDTH].reshape(NF * BLOCK, WIDTH), features, NT)
    rank_part = jnp.sum(jnp.where(same, met, 0.0).reshape(NF * CAP, RANK, MET), axis=0)
    mps[...] = rank_part.astype(BF16)
    mp_copies = [
        send(mps, mprecv.at[k], mp_s.at[k], mp_r.at[k], along_mp(o)) for k, o in enumerate(MP_OFFS)
    ]

    score_copies = []
    for c in range(4):
        here = pl.ds(64 * c, 64)
        score_copies.append(send(coded.at[here], other.at[here], sc_s.at[c], sc_r.at[c], partner))

    for copy in z_copies:
        copy.wait_recv()
    total = zsend[z]
    for k in range(1, Z):
        total = total + zrecv[k]
    xsend[...] = total
    x_copy = send(xsend, xrecv, x_s.at[0], x_r.at[0], partner)

    q_copy.wait_recv()
    other_query = expand(qother)
    upper = half == 1
    first = jnp.where(upper, other_query, own_query)
    second = jnp.where(upper, own_query, other_query)
    qfull[...] = (first + pltpu.roll(second, HALF, 1)).astype(BF16)

    for copy in mp_copies:
        copy.wait_recv()
    rank = rank_part
    for k in range(15):
        rank = rank + mprecv[k].astype(F32)
    spread = jnp.broadcast_to(rank[None], (NF * CAP, RANK, MET)).reshape(NF * BLOCK, MET)
    spread = jnp.where(same, spread, 0.0)
    up_all = facs[:, :, WIDTH : WIDTH + 128].reshape(NF * BLOCK, 128)
    coarse = spread.astype(BF16)
    rest = (spread - coarse.astype(F32)).astype(BF16)
    delta = (dot(coarse, up_all, TN) + dot(rest, up_all, TN)).reshape(NR, TOKENS, 128)
    low_m = iota((NR * 16, 128), 1) < HALF
    rets[...] = jnp.where(
        low_m, pltpu.roll(delta[:, 16:32].reshape(NR * 16, 128), HALF, 1), delta[:, 0:16].reshape(NR * 16, 128)
    ).reshape(NR, 16, 128)
    ret_copies = [
        send(rets.at[k], retrecv.at[k], ret_s.at[k], ret_r.at[k], along_dp(ROW_OFFS[k], -1))
        for k in range(1, NR)
    ]
    len_wide = jnp.pad(len_v[...].astype(F32), ((0, 0), (0, 128 - ROWS)))
    len_col = jnp.sum(
        jnp.where(iota((QROWS, 128), 1) == iota((QROWS, 128), 0) // 16, len_wide, 0.0), axis=1, keepdims=True
    )
    cache_tops, cache_sums = [], []
    for c in range(4):
        score_copies[c].wait_recv()
        here = pl.ds(64 * c, 64)
        scores = own[here, :] + decode(other[here, :])
        valid = iota((64, SLOTS), 1).astype(F32) < len_col[64 * c : 64 * c + 64]
        scores = jnp.where(valid, scores, MASKED_SCORE)
        top = jnp.max(scores, axis=1, keepdims=True)
        spread = jnp.exp(scores - top)
        cache_tops.append(top)
        cache_sums.append(jnp.sum(spread, axis=1, keepdims=True))
        spread = spread.astype(BF16)
        for r in range(4):
            ctxs[pl.ds(64 * c + 16 * r, 16), :] = dot(spread[16 * r : 16 * r + 16], cache_v[4 * c + r], NN)
    cache_top = jnp.concatenate(cache_tops, axis=0)
    cache_sum = jnp.concatenate(cache_sums, axis=0)

    x_copy.wait_recv()
    total = xsend[...] + xrecv[...]
    squares = jnp.sum(jnp.where(diagonal, total[TOKENS : TOKENS + 1, 0:128], 0.0), axis=1, keepdims=True)
    norm = lax.rsqrt(squares * (1.0 / (16 * WIDTH)) + NORM_EPSILON)
    key_lin = total[0:TOKENS, 0:128] * norm
    pair = (lane_t // 2).astype(F32)
    frequency = jnp.exp(-(2.0 * pair / (2 * HALF)) * ROPE_LOG_BASE)
    start = jnp.sum(jnp.where(lane_t == sub_t // STEPS, len_wide, 0.0), axis=1, keepdims=True)
    angle = (start + (sub_t % STEPS).astype(F32)) * frequency
    even = lane_t % 2 == 0
    turned = jnp.where(even, -pltpu.roll(key_lin, 127, 1), pltpu.roll(key_lin, 1, 1))
    key_rot = key_lin * jnp.cos(angle) + turned * jnp.sin(angle)
    new_key = key_rot.astype(BF16)
    fresh = dot(qfull[...], new_key, NT) * scale
    q_sub, t_lane = iota((QROWS, TOKENS), 0), iota((QROWS, TOKENS), 1)
    counts = (t_lane // STEPS == q_sub // 16) & (t_lane % STEPS <= (q_sub // GROUPS) % STEPS)
    fresh = jnp.where(counts, fresh, MASKED_SCORE)
    top = jnp.maximum(cache_top, jnp.max(fresh, axis=1, keepdims=True))
    fresh_exp = jnp.exp(fresh - top)
    shrink = jnp.exp(cache_top - top)
    inverse = 1.0 / (cache_sum * shrink + jnp.sum(fresh_exp, axis=1, keepdims=True))
    fresh_weights = (fresh_exp * inverse).astype(BF16)
    ctxs[...] = ctxs[...] * (shrink * inverse)
    key_own = jnp.where(upper, pltpu.roll(key_rot, HALF, 1), key_rot)
    value_base = total[0:TOKENS, 128:256]
    value_base = jnp.where(upper, value_base, pltpu.roll(value_base, HALF, 1))

    lora = rets[0]
    for copy in ret_copies:
        copy.wait_recv()
    for k in range(1, NR):
        lora = lora + retrecv[k]
    lora = jnp.concatenate([lora, pltpu.roll(lora, HALF, 1)], axis=0)

    new_value = ((value_base + 2.0 * lora) * norm).astype(BF16)
    new_ref[...] = jnp.where(low, key_own, ((value_base + 2.0 * lora) * norm)).astype(BF16)
    qexp[...] = ctxs[...] + dot(fresh_weights, new_value, NN)
    for j in range(4):
        left = qexp[pl.ds(2 * j, TOKENS, stride=GROUPS), :]
        right = qexp[pl.ds(2 * j + 1, TOKENS, stride=GROUPS), :]
        ctx_ref[:, j * 128 : j * 128 + 128] = jnp.where(low, pltpu.roll(left, HALF, 1), right).astype(BF16)

    for copy in (
        row_copies + fac_copies + z_copies + score_copies + mp_copies + ret_copies + [q_copy, x_copy]
    ):
        copy.wait_send()


def shards(
    layer_input, input_norm_gain, key_matrix, value_matrix, adapter_down_factors, adapter_up_factors,
    adapter_storage_spot, flight_adapter_ids, row_adapter_slot, lengths, queries, key_value_cache,
):
    dma = pltpu.SemaphoreType.DMA
    loads = [
        ((ROWS, STEPS, WIDTH), BF16), ((WIDTH,), BF16), ((WIDTH, 1024), BF16), ((WIDTH, 1024), BF16),
        ((64, RANK, WIDTH), BF16), ((64, RANK, HALF), BF16), ((16, 128), jnp.int32), ((1, 64), jnp.int32),
        ((1, ROWS), jnp.int32), ((1, ROWS), jnp.int32), ((ROWS, STEPS, WIDTH), BF16), ((ROWS, SLOTS, 128), BF16),
    ]
    work = [
        ((TOKENS, WIDTH), F32),
        ((QROWS, 128), F32),
        ((QROWS, 128), BF16),
        ((QROWS, 128), BF16),
        ((NR, 4 * TOKENS + 16, 128), BF16),
        ((NF, BLOCK, WIDTH + 128), BF16),
        ((Z, TOKENS + 8, 256), F32),
        ((Z, TOKENS + 8, 256), F32),
        ((TOKENS + 8, 256), F32),
        ((TOKENS + 8, 256), F32),
        ((ROWS, STEPS, WIDTH), BF16),
        ((QROWS, SLOTS), F32),
        ((QROWS, SLOTS), BF16),
        ((QROWS, SLOTS), BF16),
        ((QROWS, 128), F32),
        ((RANK, MET), BF16),
        ((15, RANK, MET), BF16),
        ((NR, 16, 128), F32),
        ((NR, 16, 128), F32),
    ]
    sems = [12, NR, NR, NF, NF, Z, Z, 1, 1, 1, 1, 4, 4, 15, 15, NR, NR]
    any_spec = pl.BlockSpec(memory_space=pl.ANY)
    vmem_spec = pl.BlockSpec(memory_space=pltpu.VMEM)
    context, newest = pl.pallas_call(
        body,
        out_shape=(
            jax.ShapeDtypeStruct((TOKENS, WIDTH), BF16),
            jax.ShapeDtypeStruct((TOKENS, 128), BF16),
        ),
        in_specs=[any_spec] * 12,
        out_specs=(vmem_spec, vmem_spec),
        scratch_shapes=[pltpu.VMEM(*s) for s in loads + work] + [dma((n,)) for n in sems],
        compiler_params=pltpu.CompilerParams(
            collective_id=0, has_side_effects=True, vmem_limit_bytes=40 * 2**20
        ),
    )(*(pltpu.with_memory_space_constraint(a, pltpu.HBM) for a in (
        layer_input,
        input_norm_gain,
        key_matrix,
        value_matrix,
        adapter_down_factors,
        adapter_up_factors,
        adapter_storage_spot.reshape(16, 128),
        flight_adapter_ids.reshape(1, 64),
        row_adapter_slot.reshape(1, ROWS),
        lengths.reshape(1, ROWS),
        queries.reshape(ROWS, STEPS, WIDTH),
        key_value_cache.reshape(ROWS, SLOTS, 128),
    )))
    return context.reshape(ROWS, STEPS, 1, WIDTH), newest.reshape(ROWS, STEPS, 1, 128)


def solution(mesh):
    return jax.shard_map(
        shards,
        mesh=mesh,
        in_specs=(
            P("dp", None, "mp"),
            P("mp"),
            P("mp", None),
            P("mp", None),
            P("dp", None, "mp"),
            P("dp", None, "mp"),
            P(),
            P(),
            P("dp", None),
            P("dp"),
            P("dp", None, "mp", None),
            P("dp", "mp", None, None),
        ),
        out_specs=(P("dp", None, "mp", None), P("dp", None, "mp", None)),
        check_vma=False,
    )
```

```python
import math

import jax
import jax.numpy as jnp
from jax import lax
from jax.experimental import pallas as pl
from jax.experimental.pallas import tpu as pltpu
from jax.sharding import PartitionSpec as P

MESH = pl.DeviceIdType.MESH
F32 = jnp.float32
BF16 = jnp.bfloat16

NORM_EPSILON = 1e-05
ROPE_LOG_BASE = math.log(500000.0)
MASKED_SCORE = -1e30

Y, Z = 8, 8
ROWS, STEPS, CAP, RANK = 16, 2, 4, 16
TOKENS = ROWS * STEPS
GROUPS, HALF, WIDTH, SLOTS = 8, 64, 512, 384
QROWS = TOKENS * GROUPS
BLOCK = CAP * RANK

ROW_OFFS = [(k, 0, 0) for k in (0, 4, 3, 5, 2, 6, 1, 7)]
FAC_OFFS = [(0, a, b) for a in range(2) for b in range(2)]
MP_OFFS = sorted(
    [(a, b) for a in range(2) for b in range(Z) if a or b], key=lambda o: -2 * o[0] - min(o[1], Z - o[1])
)
Z_OFFS = (4, 3, 5, 2, 6, 1, 7)
NR, NF = len(ROW_OFFS), len(FAC_OFFS)
MET = NR * TOKENS

NN = (((1,), (0,)), ((), ()))
NT = (((1,), (1,)), ((), ()))
TN = (((0,), (0,)), ((), ()))


def dot(a, b, dims):
    return lax.dot_general(a, b, dims, preferred_element_type=F32)


def iota(shape, axis):
    return lax.broadcasted_iota(jnp.int32, shape, axis)


CODE_RATE, CODE_SHIFT = 1.75, 124.0


def encode(score):
    power = jnp.exp2(jnp.abs(score) * CODE_RATE - CODE_SHIFT)
    return jnp.where(score < 0.0, -power, power).astype(BF16)


def decode(code):
    power = code.astype(F32)
    size = (jnp.log2(jnp.abs(power)) + CODE_SHIFT) * (1.0 / CODE_RATE)
    return jnp.where(power < 0.0, -size, size)


def body(
    x_hbm, gain_hbm, k_hbm, v_hbm, down_hbm, up_hbm, spot_hbm, ids_hbm, slot_hbm, len_hbm, q_hbm, cache_hbm,
    ctx_ref, new_ref,
    x_v, gain_v, k_v, v_v, down_v, up_v, spot_v, ids_v, slot_v, len_v, q_v, cache_v,
    flat, qexp, qown, qfull, rows, facs, zsend, zrecv, xsend, xrecv, qother,
    own, coded, other, ctxs, mps, mprecv, rets, retrecv,
    load_sem, rows_s, rows_r, facs_s, facs_r, z_s, z_r, x_s, x_r, q_s, q_r, sc_s, sc_r,
    mp_s, mp_r, ret_s, ret_r,
):
    dp, mp = lax.axis_index("dp"), lax.axis_index("mp")
    x_lo, y, core = dp // (2 * Y), (dp // 2) % Y, dp % 2
    half, z = mp // Z, mp % Z

    def along_dp(off, sign):
        to_y = (y + (Y + sign * off[0])) % Y
        return (((x_lo + off[1]) % 2) * (2 * Y) + to_y * 2 + (core + off[2]) % 2, mp)

    def along_mp(off):
        return (dp, ((half + off[0]) % 2) * Z + (z + off[1]) % Z)

    partner = (dp, (1 - half) * Z + z)

    barrier = pltpu.get_barrier_semaphore()
    greeted = [along_dp(o, 1) for o in ROW_OFFS + FAC_OFFS if o != (0, 0, 0)]
    greeted += [along_mp(o) for o in MP_OFFS]
    for device in greeted:
        pl.semaphore_signal(barrier, inc=1, device_id=device, device_id_type=MESH)

    def load(src, dst, n):
        copy = pltpu.make_async_copy(src, dst, load_sem.at[n])
        copy.start()
        return copy

    small = [
        load(x_hbm, x_v, 0), load(gain_hbm, gain_v, 1), load(spot_hbm, spot_v, 2), load(ids_hbm, ids_v, 3),
        load(slot_hbm, slot_v, 4), load(len_hbm, len_v, 5), load(q_hbm, q_v, 6),
    ]
    load_down, load_up = load(down_hbm, down_v, 7), load(up_hbm, up_v, 8)
    load_k, load_v = load(k_hbm, k_v, 9), load(v_hbm, v_v, 10)
    load_cache = load(cache_hbm, cache_v, 11)

    def send(src, dst, ss, rs, device):
        copy = pltpu.make_async_remote_copy(
            src_ref=src, dst_ref=dst, send_sem=ss, recv_sem=rs, device_id=device, device_id_type=MESH
        )
        copy.start()
        return copy

    for copy in small:
        copy.wait()

    for r in range(ROWS):
        flat[pl.ds(2 * r, 2), :] = x_v[r].astype(F32)
    hidden = flat[...]
    gained = (hidden * gain_v[...].astype(F32).reshape(1, WIDTH)).astype(BF16)
    for j in range(4):
        rows[0, TOKENS * j : TOKENS * j + TOKENS, :] = gained[:, 128 * j : 128 * j + 128]
    square = jnp.sum(hidden * hidden, axis=1, keepdims=True)
    lane_t, sub_t = iota((TOKENS, 128), 1), iota((TOKENS, 128), 0)
    diagonal = lane_t == sub_t
    square_row = jnp.sum(jnp.where(diagonal, square, 0.0), axis=0, keepdims=True)

    sub16, lane16 = iota((ROWS, 128), 0), iota((ROWS, 128), 1)
    slot_wide = jnp.pad(slot_v[...].astype(F32), ((0, 0), (0, 128 - ROWS)))
    slot_col = jnp.sum(jnp.where(sub16 == lane16, slot_wide, 0.0), axis=1, keepdims=True)
    tag_row = jnp.sum(
        jnp.where(sub16 == (lane16 % TOKENS) // STEPS, slot_col, 0.0), axis=0, keepdims=True
    )
    rows[0, 4 * TOKENS : 4 * TOKENS + 16, :] = jnp.broadcast_to(tag_row, (16, 128)).astype(BF16)

    pl.semaphore_wait(barrier, len(greeted))

    row_copies = [
        send(rows.at[0], rows.at[k], rows_s.at[k], rows_r.at[k], along_dp(ROW_OFFS[k], 1)) for k in range(1, NR)
    ]
    sub64, lane64 = iota((64, 64), 0), iota((64, 64), 1)
    ids_col = jnp.sum(jnp.where(sub64 == lane64, ids_v[...].astype(F32), 0.0), axis=1, keepdims=True)
    spots = spot_v[...].astype(F32)
    lane_n = iota((64, 128), 1).astype(F32)
    found = jnp.zeros((64, 128), F32)
    for i in range(16):
        found = found + jnp.where(ids_col - (128.0 * i) == lane_n, spots[i : i + 1, :], 0.0)
    place_col = jnp.sum(found, axis=1, keepdims=True)
    place_row = jnp.sum(jnp.where(sub64 == lane64, place_col, 0.0), axis=0, keepdims=True)
    group = dp.astype(F32)
    owner_row = jnp.floor(place_row * (1.0 / 64))
    mine_row = jnp.where(owner_row == group, 1.0, 0.0)
    mine_col = jnp.where(jnp.floor(place_col * (1.0 / 64)) == group, 1.0, 0.0)
    order_row = jnp.sum(jnp.where(sub64 < lane64, mine_col, 0.0), axis=0, keepdims=True)
    sub_f = (sub64 // RANK).astype(F32)
    picks = jnp.where(order_row == sub_f, mine_row, 0.0)
    target = jnp.sum(picks * (place_row - 64.0 * owner_row), axis=1, keepdims=True) * RANK
    target = target + (iota((64, 1), 0) % RANK).astype(F32)
    tag_col = jnp.sum(picks * (lane64 + 1).astype(F32), axis=1, keepdims=True) - 1.0
    select = jnp.where(target == iota((64, 1024), 1).astype(F32), 1.0, 0.0).astype(BF16)

    load_down.wait()
    facs[0, :, 0:WIDTH] = dot(select, down_v[...].reshape(64 * RANK, WIDTH), NN).astype(BF16)
    load_up.wait()
    up_own = dot(select, up_v[...].reshape(64 * RANK, HALF), NN).astype(BF16)
    shift = jnp.where(iota((HALF, 128), 1) == iota((HALF, 128), 0) + HALF, 1.0, 0.0).astype(BF16)
    up_wide = dot(up_own, shift, NN)
    facs[0, :, WIDTH : WIDTH + 128] = jnp.where(iota((64, 128), 1) < HALF, tag_col, up_wide).astype(BF16)

    fac_copies = [
        send(facs.at[0], facs.at[k], facs_s.at[k], facs_r.at[k], along_dp(FAC_OFFS[k], 1)) for k in range(1, NF)
    ]
    q_copy = send(q_v, qother, q_s.at[0], q_r.at[0], partner)

    low = lane_t < HALF
    square_rows = jnp.broadcast_to(square_row, (8, 128))
    for w, (copy, weight) in enumerate(((load_k, k_v), (load_v, v_v))):
        copy.wait()
        part = dot(gained, weight[...], NN)
        here = slice(w * 128, w * 128 + 128)
        for j in range(4):
            first = part[:, j * 128 : j * 128 + 128]
            second = part[:, 512 + j * 128 : 512 + j * 128 + 128]
            zsend[2 * j, 0:TOKENS, here] = jnp.where(low, first, pltpu.roll(second, HALF, 1))
            zsend[2 * j + 1, 0:TOKENS, here] = jnp.where(low, pltpu.roll(first, HALF, 1), second)
        for j in range(Z):
            zsend[j, TOKENS : TOKENS + 8, here] = square_rows
    z_copies = [
        send(zsend.at[(z + k) % Z], zrecv.at[k], z_s.at[k], z_r.at[k], along_mp((0, k))) for k in Z_OFFS
    ]

    def expand(ref):
        for r in range(ROWS):
            flat[pl.ds(2 * r, 2), :] = ref[r].astype(F32)
        for g in range(GROUPS):
            tile = flat[:, (g // 2) * 128 : (g // 2) * 128 + 128]
            if g % 2:
                tile = pltpu.roll(tile, HALF, 1)
            qexp[pl.ds(g, TOKENS, stride=GROUPS), :] = jnp.where(low, tile, 0.0)
        return qexp[...]

    scale = 1.0 / math.sqrt(2 * HALF)
    own_query = expand(q_v)
    qown[...] = own_query.astype(BF16)
    load_cache.wait()
    for r in range(ROWS):
        here = pl.ds(16 * r, 16)
        piece = dot(qown[here, :], cache_v[r], NT) * scale
        own[here, :] = piece
        coded[here, :] = encode(piece)

    for copy in row_copies + fac_copies:
        copy.wait_recv()
    lane_r = iota((16, 128), 1)
    tag_tiles = []
    for j in range((NR + 3) // 4):
        tile = jnp.zeros((16, 128), F32)
        for k in range(4 * j, min(4 * j + 4, NR)):
            tile = jnp.where(lane_r // TOKENS == k % 4, rows[k, 4 * TOKENS : 4 * TOKENS + 16, :].astype(F32), tile)
        tag_tiles.append(tile)
    tag_all = jnp.concatenate(tag_tiles, axis=1)[0:1, :MET]
    fac_tag = facs[:, :, WIDTH : WIDTH + 128].reshape(NF * BLOCK, 128)[:, 0:1].astype(F32)
    same = fac_tag == tag_all
    features = jnp.concatenate(
        [rows[:, TOKENS * j : TOKENS * j + TOKENS, :].reshape(MET, 128) for j in range(4)], axis=1
    )
    met = dot(facs[:, :, 0:WIDTH].reshape(NF * BLOCK, WIDTH), features, NT)
    rank_part = jnp.sum(jnp.where(same, met, 0.0).reshape(NF * CAP, RANK, MET), axis=0)
    mps[...] = rank_part.astype(BF16)
    mp_copies = [
        send(mps, mprecv.at[k], mp_s.at[k], mp_r.at[k], along_mp(o)) for k, o in enumerate(MP_OFFS)
    ]

    score_copies = []
    for c in range(4):
        here = pl.ds(64 * c, 64)
        score_copies.append(send(coded.at[here], other.at[here], sc_s.at[c], sc_r.at[c], partner))

    for copy in z_copies:
        copy.wait_recv()
    total = zsend[z]
    for k in range(1, Z):
        total = total + zrecv[k]
    xsend[...] = total
    x_copy = send(xsend, xrecv, x_s.at[0], x_r.at[0], partner)

    q_copy.wait_recv()
    other_query = expand(qother)
    upper = half == 1
    first = jnp.where(upper, other_query, own_query)
    second = jnp.where(upper, own_query, other_query)
    qfull[...] = (first + pltpu.roll(second, HALF, 1)).astype(BF16)

    for copy in mp_copies:
        copy.wait_recv()
    rank = rank_part
    for k in range(15):
        rank = rank + mprecv[k].astype(F32)
    spread = jnp.broadcast_to(rank[None], (NF * CAP, RANK, MET)).reshape(NF * BLOCK, MET)
    spread = jnp.where(same, spread, 0.0)
    up_all = facs[:, :, WIDTH : WIDTH + 128].reshape(NF * BLOCK, 128)
    coarse = spread.astype(BF16)
    rest = (spread - coarse.astype(F32)).astype(BF16)
    delta = (dot(coarse, up_all, TN) + dot(rest, up_all, TN)).reshape(NR, TOKENS, 128)
    low_m = iota((NR * 16, 128), 1) < HALF
    rets[...] = jnp.where(
        low_m, pltpu.roll(delta[:, 16:32].reshape(NR * 16, 128), HALF, 1), delta[:, 0:16].reshape(NR * 16, 128)
    ).reshape(NR, 16, 128)
    ret_copies = [
        send(rets.at[k], retrecv.at[k], ret_s.at[k], ret_r.at[k], along_dp(ROW_OFFS[k], -1))
        for k in range(1, NR)
    ]
    len_wide = jnp.pad(len_v[...].astype(F32), ((0, 0), (0, 128 - ROWS)))
    len_col = jnp.sum(
        jnp.where(iota((QROWS, 128), 1) == iota((QROWS, 128), 0) // 16, len_wide, 0.0), axis=1, keepdims=True
    )
    cache_tops, cache_sums = [], []
    for c in range(4):
        score_copies[c].wait_recv()
        here = pl.ds(64 * c, 64)
        scores = own[here, :] + decode(other[here, :])
        valid = iota((64, SLOTS), 1).astype(F32) < len_col[64 * c : 64 * c + 64]
        scores = jnp.where(valid, scores, MASKED_SCORE)
        top = jnp.max(scores, axis=1, keepdims=True)
        spread = jnp.exp(scores - top)
        cache_tops.append(top)
        cache_sums.append(jnp.sum(spread, axis=1, keepdims=True))
        spread = spread.astype(BF16)
        for r in range(4):
            ctxs[pl.ds(64 * c + 16 * r, 16), :] = dot(spread[16 * r : 16 * r + 16], cache_v[4 * c + r], NN)
    cache_top = jnp.concatenate(cache_tops, axis=0)
    cache_sum = jnp.concatenate(cache_sums, axis=0)

    x_copy.wait_recv()
    total = xsend[...] + xrecv[...]
    squares = jnp.sum(jnp.where(diagonal, total[TOKENS : TOKENS + 1, 0:128], 0.0), axis=1, keepdims=True)
    norm = lax.rsqrt(squares * (1.0 / (16 * WIDTH)) + NORM_EPSILON)
    key_lin = total[0:TOKENS, 0:128] * norm
    pair = (lane_t // 2).astype(F32)
    frequency = jnp.exp(-(2.0 * pair / (2 * HALF)) * ROPE_LOG_BASE)
    start = jnp.sum(jnp.where(lane_t == sub_t // STEPS, len_wide, 0.0), axis=1, keepdims=True)
    angle = (start + (sub_t % STEPS).astype(F32)) * frequency
    even = lane_t % 2 == 0
    turned = jnp.where(even, -pltpu.roll(key_lin, 127, 1), pltpu.roll(key_lin, 1, 1))
    key_rot = key_lin * jnp.cos(angle) + turned * jnp.sin(angle)
    new_key = key_rot.astype(BF16)
    fresh = dot(qfull[...], new_key, NT) * scale
    q_sub, t_lane = iota((QROWS, TOKENS), 0), iota((QROWS, TOKENS), 1)
    counts = (t_lane // STEPS == q_sub // 16) & (t_lane % STEPS <= (q_sub // GROUPS) % STEPS)
    fresh = jnp.where(counts, fresh, MASKED_SCORE)
    top = jnp.maximum(cache_top, jnp.max(fresh, axis=1, keepdims=True))
    fresh_exp = jnp.exp(fresh - top)
    shrink = jnp.exp(cache_top - top)
    inverse = 1.0 / (cache_sum * shrink + jnp.sum(fresh_exp, axis=1, keepdims=True))
    fresh_weights = (fresh_exp * inverse).astype(BF16)
    ctxs[...] = ctxs[...] * (shrink * inverse)
    key_own = jnp.where(upper, pltpu.roll(key_rot, HALF, 1), key_rot)
    value_base = total[0:TOKENS, 128:256]
    value_base = jnp.where(upper, value_base, pltpu.roll(value_base, HALF, 1))

    lora = rets[0]
    for copy in ret_copies:
        copy.wait_recv()
    for k in range(1, NR):
        lora = lora + retrecv[k]
    lora = jnp.concatenate([lora, pltpu.roll(lora, HALF, 1)], axis=0)

    new_value = ((value_base + 2.0 * lora) * norm).astype(BF16)
    flat[:, 0:128] = jnp.where(low, key_own, (value_base + 2.0 * lora) * norm)
    for r in range(ROWS):
        new_ref[r] = flat[pl.ds(2 * r, 2), 0:128].astype(BF16)
    qexp[...] = ctxs[...] + dot(fresh_weights, new_value, NN)
    for j in range(4):
        left = qexp[pl.ds(2 * j, TOKENS, stride=GROUPS), :]
        right = qexp[pl.ds(2 * j + 1, TOKENS, stride=GROUPS), :]
        flat[:, j * 128 : j * 128 + 128] = jnp.where(low, pltpu.roll(left, HALF, 1), right)
    for r in range(ROWS):
        ctx_ref[r] = flat[pl.ds(2 * r, 2), :].astype(BF16)

    for copy in (
        row_copies + fac_copies + z_copies + score_copies + mp_copies + ret_copies + [q_copy, x_copy]
    ):
        copy.wait_send()


def place(ctx_ref, new_ref, ctx_out, new_out, sem):
    first = pltpu.make_async_copy(ctx_ref, ctx_out, sem.at[0])
    second = pltpu.make_async_copy(new_ref, new_out, sem.at[1])
    first.start()
    second.start()
    first.wait()
    second.wait()


def shards(
    layer_input, input_norm_gain, key_matrix, value_matrix, adapter_down_factors, adapter_up_factors,
    adapter_storage_spot, flight_adapter_ids, row_adapter_slot, lengths, queries, key_value_cache,
):
    dma = pltpu.SemaphoreType.DMA
    loads = [
        ((ROWS, STEPS, WIDTH), BF16), ((WIDTH,), BF16), ((WIDTH, 1024), BF16), ((WIDTH, 1024), BF16),
        ((64, RANK, WIDTH), BF16), ((64, RANK, HALF), BF16), ((16, 128), jnp.int32), ((1, 64), jnp.int32),
        ((1, ROWS), jnp.int32), ((1, ROWS), jnp.int32), ((ROWS, STEPS, WIDTH), BF16), ((ROWS, SLOTS, 128), BF16),
    ]
    work = [
        ((TOKENS, WIDTH), F32),
        ((QROWS, 128), F32),
        ((QROWS, 128), BF16),
        ((QROWS, 128), BF16),
        ((NR, 4 * TOKENS + 16, 128), BF16),
        ((NF, BLOCK, WIDTH + 128), BF16),
        ((Z, TOKENS + 8, 256), F32),
        ((Z, TOKENS + 8, 256), F32),
        ((TOKENS + 8, 256), F32),
        ((TOKENS + 8, 256), F32),
        ((ROWS, STEPS, WIDTH), BF16),
        ((QROWS, SLOTS), F32),
        ((QROWS, SLOTS), BF16),
        ((QROWS, SLOTS), BF16),
        ((QROWS, 128), F32),
        ((RANK, MET), BF16),
        ((15, RANK, MET), BF16),
        ((NR, 16, 128), F32),
        ((NR, 16, 128), F32),
    ]
    sems = [12, NR, NR, NF, NF, Z, Z, 1, 1, 1, 1, 4, 4, 15, 15, NR, NR]
    any_spec = pl.BlockSpec(memory_space=pl.ANY)
    vmem_spec = pl.BlockSpec(memory_space=pltpu.VMEM)
    context, newest = pl.pallas_call(
        body,
        out_shape=(
            jax.ShapeDtypeStruct((ROWS, STEPS, WIDTH), BF16),
            jax.ShapeDtypeStruct((ROWS, STEPS, 128), BF16),
        ),
        in_specs=[any_spec] * 12,
        out_specs=(vmem_spec, vmem_spec),
        scratch_shapes=[pltpu.VMEM(*s) for s in loads + work] + [dma((n,)) for n in sems],
        compiler_params=pltpu.CompilerParams(
            collective_id=0, has_side_effects=True, vmem_limit_bytes=40 * 2**20
        ),
    )(*(pltpu.with_memory_space_constraint(a, pltpu.HBM) for a in (
        layer_input,
        input_norm_gain,
        key_matrix,
        value_matrix,
        adapter_down_factors,
        adapter_up_factors,
        adapter_storage_spot.reshape(16, 128),
        flight_adapter_ids.reshape(1, 64),
        row_adapter_slot.reshape(1, ROWS),
        lengths.reshape(1, ROWS),
        queries.reshape(ROWS, STEPS, WIDTH),
        key_value_cache.reshape(ROWS, SLOTS, 128),
    )))
    context, newest = pl.pallas_call(
        place,
        out_shape=(
            pltpu.HBM((ROWS, STEPS, WIDTH), BF16),
            pltpu.HBM((ROWS, STEPS, 128), BF16),
        ),
        in_specs=[any_spec, any_spec],
        out_specs=(any_spec, any_spec),
        scratch_shapes=[dma((2,))],
    )(pltpu.with_memory_space_constraint(context, pltpu.VMEM), pltpu.with_memory_space_constraint(newest, pltpu.VMEM))
    return context.reshape(ROWS, STEPS, 1, WIDTH), newest.reshape(ROWS, STEPS, 1, 128)


def solution(mesh):
    return jax.shard_map(
        shards,
        mesh=mesh,
        in_specs=(
            P("dp", None, "mp"),
            P("mp"),
            P("mp", None),
            P("mp", None),
            P("dp", None, "mp"),
            P("dp", None, "mp"),
            P(),
            P(),
            P("dp", None),
            P("dp"),
            P("dp", None, "mp", None),
            P("dp", "mp", None, None),
        ),
        out_specs=(P("dp", None, "mp", None), P("dp", None, "mp", None)),
        check_vma=False,
    )
```

```python
import math

import jax
import jax.numpy as jnp
from jax import lax
from jax.experimental import pallas as pl
from jax.experimental.pallas import tpu as pltpu
from jax.sharding import PartitionSpec as P

MESH = pl.DeviceIdType.MESH
F32 = jnp.float32
BF16 = jnp.bfloat16

NORM_EPSILON = 1e-05
ROPE_LOG_BASE = math.log(500000.0)
MASKED_SCORE = -1e30

Y, Z = 8, 8
ROWS, STEPS, CAP, RANK = 16, 2, 4, 16
TOKENS = ROWS * STEPS
GROUPS, HALF, WIDTH, SLOTS = 8, 64, 512, 384
QROWS = TOKENS * GROUPS
BLOCK = CAP * RANK

ROW_OFFS = [(k, 0, 0) for k in (0, 4, 3, 5, 2, 6, 1, 7)]
FAC_OFFS = [(0, a, b) for a in range(2) for b in range(2)]
MP_OFFS = sorted(
    [(a, b) for a in range(2) for b in range(Z) if a or b], key=lambda o: -2 * o[0] - min(o[1], Z - o[1])
)
Z_OFFS = (4, 3, 5, 2, 6, 1, 7)
NR, NF = len(ROW_OFFS), len(FAC_OFFS)
MET = NR * TOKENS

NN = (((1,), (0,)), ((), ()))
NT = (((1,), (1,)), ((), ()))
TN = (((0,), (0,)), ((), ()))


def dot(a, b, dims):
    return lax.dot_general(a, b, dims, preferred_element_type=F32)


def iota(shape, axis):
    return lax.broadcasted_iota(jnp.int32, shape, axis)


CODE_RATE, CODE_SHIFT = 1.75, 124.0


def encode(score):
    power = jnp.exp2(jnp.abs(score) * CODE_RATE - CODE_SHIFT)
    return jnp.where(score < 0.0, -power, power).astype(BF16)


def decode(code):
    power = code.astype(F32)
    size = (jnp.log2(jnp.abs(power)) + CODE_SHIFT) * (1.0 / CODE_RATE)
    return jnp.where(power < 0.0, -size, size)


def body(
    x_hbm, gain_hbm, k_hbm, v_hbm, down_hbm, up_hbm, spot_hbm, ids_hbm, slot_hbm, len_hbm, q_hbm, cache_hbm,
    ctx_ref, new_ref,
    x_v, gain_v, k_v, v_v, down_v, up_v, spot_v, ids_v, slot_v, len_v, q_v, cache_v,
    flat, qexp, qown, qfull, rows, facs, zsend, zrecv, xsend, xrecv, qother,
    own, coded, other, ctxs, mps, mprecv, rets, retrecv,
    load_sem, rows_s, rows_r, facs_s, facs_r, z_s, z_r, x_s, x_r, q_s, q_r, sc_s, sc_r,
    mp_s, mp_r, ret_s, ret_r,
):
    dp, mp = lax.axis_index("dp"), lax.axis_index("mp")
    x_lo, y, core = dp // (2 * Y), (dp // 2) % Y, dp % 2
    half, z = mp // Z, mp % Z

    def along_dp(off, sign):
        to_y = (y + (Y + sign * off[0])) % Y
        return (((x_lo + off[1]) % 2) * (2 * Y) + to_y * 2 + (core + off[2]) % 2, mp)

    def along_mp(off):
        return (dp, ((half + off[0]) % 2) * Z + (z + off[1]) % Z)

    partner = (dp, (1 - half) * Z + z)

    barrier = pltpu.get_barrier_semaphore()
    greeted = [along_dp(o, 1) for o in ROW_OFFS + FAC_OFFS if o != (0, 0, 0)]
    greeted += [along_mp(o) for o in MP_OFFS]
    for device in greeted:
        pl.semaphore_signal(barrier, inc=1, device_id=device, device_id_type=MESH)

    def load(src, dst, n):
        copy = pltpu.make_async_copy(src, dst, load_sem.at[n])
        copy.start()
        return copy

    small = [
        load(x_hbm, x_v, 0), load(gain_hbm, gain_v, 1), load(spot_hbm, spot_v, 2), load(ids_hbm, ids_v, 3),
        load(slot_hbm, slot_v, 4), load(len_hbm, len_v, 5), load(q_hbm, q_v, 6),
    ]
    load_down, load_up = load(down_hbm, down_v, 7), load(up_hbm, up_v, 8)
    load_k, load_v = load(k_hbm, k_v, 9), load(v_hbm, v_v, 10)
    load_cache = load(cache_hbm, cache_v, 11)

    def send(src, dst, ss, rs, device):
        copy = pltpu.make_async_remote_copy(
            src_ref=src, dst_ref=dst, send_sem=ss, recv_sem=rs, device_id=device, device_id_type=MESH
        )
        copy.start()
        return copy

    for copy in small:
        copy.wait()

    for r in range(ROWS):
        flat[pl.ds(2 * r, 2), :] = x_v[r].astype(F32)
    hidden = flat[...]
    gained = (hidden * gain_v[...].astype(F32).reshape(1, WIDTH)).astype(BF16)
    for j in range(4):
        rows[0, TOKENS * j : TOKENS * j + TOKENS, :] = gained[:, 128 * j : 128 * j + 128]
    square = jnp.sum(hidden * hidden, axis=1, keepdims=True)
    lane_t, sub_t = iota((TOKENS, 128), 1), iota((TOKENS, 128), 0)
    diagonal = lane_t == sub_t
    square_row = jnp.sum(jnp.where(diagonal, square, 0.0), axis=0, keepdims=True)

    sub16, lane16 = iota((ROWS, 128), 0), iota((ROWS, 128), 1)
    slot_wide = jnp.pad(slot_v[...].astype(F32), ((0, 0), (0, 128 - ROWS)))
    slot_col = jnp.sum(jnp.where(sub16 == lane16, slot_wide, 0.0), axis=1, keepdims=True)
    tag_row = jnp.sum(
        jnp.where(sub16 == (lane16 % TOKENS) // STEPS, slot_col, 0.0), axis=0, keepdims=True
    )
    rows[0, 4 * TOKENS : 4 * TOKENS + 16, :] = jnp.broadcast_to(tag_row, (16, 128)).astype(BF16)

    pl.semaphore_wait(barrier, len(greeted))

    row_copies = [
        send(rows.at[0], rows.at[k], rows_s.at[k], rows_r.at[k], along_dp(ROW_OFFS[k], 1)) for k in range(1, NR)
    ]
    sub64, lane64 = iota((64, 64), 0), iota((64, 64), 1)
    ids_col = jnp.sum(jnp.where(sub64 == lane64, ids_v[...].astype(F32), 0.0), axis=1, keepdims=True)
    spots = spot_v[...].astype(F32)
    lane_n = iota((64, 128), 1).astype(F32)
    found = jnp.zeros((64, 128), F32)
    for i in range(16):
        found = found + jnp.where(ids_col - (128.0 * i) == lane_n, spots[i : i + 1, :], 0.0)
    place_col = jnp.sum(found, axis=1, keepdims=True)
    place_row = jnp.sum(jnp.where(sub64 == lane64, place_col, 0.0), axis=0, keepdims=True)
    group = dp.astype(F32)
    owner_row = jnp.floor(place_row * (1.0 / 64))
    mine_row = jnp.where(owner_row == group, 1.0, 0.0)
    mine_col = jnp.where(jnp.floor(place_col * (1.0 / 64)) == group, 1.0, 0.0)
    order_row = jnp.sum(jnp.where(sub64 < lane64, mine_col, 0.0), axis=0, keepdims=True)
    sub_f = (sub64 // RANK).astype(F32)
    picks = jnp.where(order_row == sub_f, mine_row, 0.0)
    target = jnp.sum(picks * (place_row - 64.0 * owner_row), axis=1, keepdims=True) * RANK
    target = target + (iota((64, 1), 0) % RANK).astype(F32)
    tag_col = jnp.sum(picks * (lane64 + 1).astype(F32), axis=1, keepdims=True) - 1.0
    select = jnp.where(target == iota((64, 1024), 1).astype(F32), 1.0, 0.0).astype(BF16)

    load_down.wait()
    facs[0, :, 0:WIDTH] = dot(select, down_v[...].reshape(64 * RANK, WIDTH), NN).astype(BF16)
    load_up.wait()
    up_own = dot(select, up_v[...].reshape(64 * RANK, HALF), NN).astype(BF16)
    shift = jnp.where(iota((HALF, 128), 1) == iota((HALF, 128), 0) + HALF, 1.0, 0.0).astype(BF16)
    up_wide = dot(up_own, shift, NN)
    facs[0, :, WIDTH : WIDTH + 128] = jnp.where(iota((64, 128), 1) < HALF, tag_col, up_wide).astype(BF16)

    fac_copies = [
        send(facs.at[0], facs.at[k], facs_s.at[k], facs_r.at[k], along_dp(FAC_OFFS[k], 1)) for k in range(1, NF)
    ]
    q_copy = send(q_v, qother, q_s.at[0], q_r.at[0], partner)

    low = lane_t < HALF
    square_rows = jnp.broadcast_to(square_row, (8, 128))
    for w, (copy, weight) in enumerate(((load_k, k_v), (load_v, v_v))):
        copy.wait()
        part = dot(gained, weight[...], NN)
        here = slice(w * 128, w * 128 + 128)
        for j in range(4):
            first = part[:, j * 128 : j * 128 + 128]
            second = part[:, 512 + j * 128 : 512 + j * 128 + 128]
            zsend[2 * j, 0:TOKENS, here] = jnp.where(low, first, pltpu.roll(second, HALF, 1))
            zsend[2 * j + 1, 0:TOKENS, here] = jnp.where(low, pltpu.roll(first, HALF, 1), second)
        for j in range(Z):
            zsend[j, TOKENS : TOKENS + 8, here] = square_rows
    z_copies = [
        send(zsend.at[(z + k) % Z], zrecv.at[k], z_s.at[k], z_r.at[k], along_mp((0, k))) for k in Z_OFFS
    ]

    def expand(ref):
        for r in range(ROWS):
            flat[pl.ds(2 * r, 2), :] = ref[r].astype(F32)
        for g in range(GROUPS):
            tile = flat[:, (g // 2) * 128 : (g // 2) * 128 + 128]
            if g % 2:
                tile = pltpu.roll(tile, HALF, 1)
            qexp[pl.ds(g, TOKENS, stride=GROUPS), :] = jnp.where(low, tile, 0.0)
        return qexp[...]

    scale = 1.0 / math.sqrt(2 * HALF)
    own_query = expand(q_v)
    qown[...] = own_query.astype(BF16)
    load_cache.wait()
    for r in range(ROWS):
        here = pl.ds(16 * r, 16)
        piece = dot(qown[here, :], cache_v[r], NT) * scale
        own[here, :] = piece
        coded[here, :] = encode(piece)

    score_copies = []
    for c in range(0, 2):
        here = pl.ds(64 * c, 64)
        score_copies.append(send(coded.at[here], other.at[here], sc_s.at[c], sc_r.at[c], partner))

    for copy in row_copies + fac_copies:
        copy.wait_recv()
    lane_r = iota((16, 128), 1)
    tag_tiles = []
    for j in range((NR + 3) // 4):
        tile = jnp.zeros((16, 128), F32)
        for k in range(4 * j, min(4 * j + 4, NR)):
            tile = jnp.where(lane_r // TOKENS == k % 4, rows[k, 4 * TOKENS : 4 * TOKENS + 16, :].astype(F32), tile)
        tag_tiles.append(tile)
    tag_all = jnp.concatenate(tag_tiles, axis=1)[0:1, :MET]
    fac_tag = facs[:, :, WIDTH : WIDTH + 128].reshape(NF * BLOCK, 128)[:, 0:1].astype(F32)
    same = fac_tag == tag_all
    features = jnp.concatenate(
        [rows[:, TOKENS * j : TOKENS * j + TOKENS, :].reshape(MET, 128) for j in range(4)], axis=1
    )
    met = dot(facs[:, :, 0:WIDTH].reshape(NF * BLOCK, WIDTH), features, NT)
    rank_part = jnp.sum(jnp.where(same, met, 0.0).reshape(NF * CAP, RANK, MET), axis=0)
    mps[...] = rank_part.astype(BF16)
    mp_copies = [
        send(mps, mprecv.at[k], mp_s.at[k], mp_r.at[k], along_mp(o)) for k, o in enumerate(MP_OFFS)
    ]

    for c in range(2, 4):
        here = pl.ds(64 * c, 64)
        score_copies.append(send(coded.at[here], other.at[here], sc_s.at[c], sc_r.at[c], partner))

    for copy in z_copies:
        copy.wait_recv()
    total = zsend[z]
    for k in range(1, Z):
        total = total + zrecv[k]
    xsend[...] = total
    x_copy = send(xsend, xrecv, x_s.at[0], x_r.at[0], partner)

    q_copy.wait_recv()
    other_query = expand(qother)
    upper = half == 1
    first = jnp.where(upper, other_query, own_query)
    second = jnp.where(upper, own_query, other_query)
    qfull[...] = (first + pltpu.roll(second, HALF, 1)).astype(BF16)

    for copy in mp_copies:
        copy.wait_recv()
    rank = rank_part
    for k in range(15):
        rank = rank + mprecv[k].astype(F32)
    spread = jnp.broadcast_to(rank[None], (NF * CAP, RANK, MET)).reshape(NF * BLOCK, MET)
    spread = jnp.where(same, spread, 0.0)
    up_all = facs[:, :, WIDTH : WIDTH + 128].reshape(NF * BLOCK, 128)
    coarse = spread.astype(BF16)
    rest = (spread - coarse.astype(F32)).astype(BF16)
    delta = (dot(coarse, up_all, TN) + dot(rest, up_all, TN)).reshape(NR, TOKENS, 128)
    low_m = iota((NR * 16, 128), 1) < HALF
    rets[...] = jnp.where(
        low_m, pltpu.roll(delta[:, 16:32].reshape(NR * 16, 128), HALF, 1), delta[:, 0:16].reshape(NR * 16, 128)
    ).reshape(NR, 16, 128).astype(BF16)
    ret_copies = [
        send(rets.at[k], retrecv.at[k], ret_s.at[k], ret_r.at[k], along_dp(ROW_OFFS[k], -1))
        for k in range(1, NR)
    ]
    len_wide = jnp.pad(len_v[...].astype(F32), ((0, 0), (0, 128 - ROWS)))
    len_col = jnp.sum(
        jnp.where(iota((QROWS, 128), 1) == iota((QROWS, 128), 0) // 16, len_wide, 0.0), axis=1, keepdims=True
    )
    cache_tops, cache_sums = [], []
    for c in range(4):
        score_copies[c].wait_recv()
        here = pl.ds(64 * c, 64)
        scores = own[here, :] + decode(other[here, :])
        valid = iota((64, SLOTS), 1).astype(F32) < len_col[64 * c : 64 * c + 64]
        scores = jnp.where(valid, scores, MASKED_SCORE)
        top = jnp.max(scores, axis=1, keepdims=True)
        spread = jnp.exp(scores - top)
        cache_tops.append(top)
        cache_sums.append(jnp.sum(spread, axis=1, keepdims=True))
        spread = spread.astype(BF16)
        for r in range(4):
            ctxs[pl.ds(64 * c + 16 * r, 16), :] = dot(spread[16 * r : 16 * r + 16], cache_v[4 * c + r], NN)
    cache_top = jnp.concatenate(cache_tops, axis=0)
    cache_sum = jnp.concatenate(cache_sums, axis=0)

    x_copy.wait_recv()
    total = xsend[...] + xrecv[...]
    squares = jnp.sum(jnp.where(diagonal, total[TOKENS : TOKENS + 1, 0:128], 0.0), axis=1, keepdims=True)
    norm = lax.rsqrt(squares * (1.0 / (16 * WIDTH)) + NORM_EPSILON)
    key_lin = total[0:TOKENS, 0:128] * norm
    pair = (lane_t // 2).astype(F32)
    frequency = jnp.exp(-(2.0 * pair / (2 * HALF)) * ROPE_LOG_BASE)
    start = jnp.sum(jnp.where(lane_t == sub_t // STEPS, len_wide, 0.0), axis=1, keepdims=True)
    angle = (start + (sub_t % STEPS).astype(F32)) * frequency
    even = lane_t % 2 == 0
    turned = jnp.where(even, -pltpu.roll(key_lin, 127, 1), pltpu.roll(key_lin, 1, 1))
    key_rot = key_lin * jnp.cos(angle) + turned * jnp.sin(angle)
    new_key = key_rot.astype(BF16)
    fresh = dot(qfull[...], new_key, NT) * scale
    q_sub, t_lane = iota((QROWS, TOKENS), 0), iota((QROWS, TOKENS), 1)
    counts = (t_lane // STEPS == q_sub // 16) & (t_lane % STEPS <= (q_sub // GROUPS) % STEPS)
    fresh = jnp.where(counts, fresh, MASKED_SCORE)
    top = jnp.maximum(cache_top, jnp.max(fresh, axis=1, keepdims=True))
    fresh_exp = jnp.exp(fresh - top)
    shrink = jnp.exp(cache_top - top)
    inverse = 1.0 / (cache_sum * shrink + jnp.sum(fresh_exp, axis=1, keepdims=True))
    fresh_weights = (fresh_exp * inverse).astype(BF16)
    ctxs[...] = ctxs[...] * (shrink * inverse)
    key_own = jnp.where(upper, pltpu.roll(key_rot, HALF, 1), key_rot)
    value_base = total[0:TOKENS, 128:256]
    value_base = jnp.where(upper, value_base, pltpu.roll(value_base, HALF, 1))

    lora = rets[0].astype(F32)
    for copy in ret_copies:
        copy.wait_recv()
    for k in range(1, NR):
        lora = lora + retrecv[k].astype(F32)
    lora = jnp.concatenate([lora, pltpu.roll(lora, HALF, 1)], axis=0)

    new_value = ((value_base + 2.0 * lora) * norm).astype(BF16)
    flat[:, 0:128] = jnp.where(low, key_own, (value_base + 2.0 * lora) * norm)
    for r in range(ROWS):
        new_ref[r] = flat[pl.ds(2 * r, 2), 0:128].astype(BF16)
    qexp[...] = ctxs[...] + dot(fresh_weights, new_value, NN)
    for j in range(4):
        left = qexp[pl.ds(2 * j, TOKENS, stride=GROUPS), :]
        right = qexp[pl.ds(2 * j + 1, TOKENS, stride=GROUPS), :]
        flat[:, j * 128 : j * 128 + 128] = jnp.where(low, pltpu.roll(left, HALF, 1), right)
    for r in range(ROWS):
        ctx_ref[r] = flat[pl.ds(2 * r, 2), :].astype(BF16)

    for copy in (
        row_copies + fac_copies + z_copies + score_copies + mp_copies + ret_copies + [q_copy, x_copy]
    ):
        copy.wait_send()


def place(ctx_ref, new_ref, ctx_out, new_out, sem):
    first = pltpu.make_async_copy(ctx_ref, ctx_out, sem.at[0])
    second = pltpu.make_async_copy(new_ref, new_out, sem.at[1])
    first.start()
    second.start()
    first.wait()
    second.wait()


def shards(
    layer_input, input_norm_gain, key_matrix, value_matrix, adapter_down_factors, adapter_up_factors,
    adapter_storage_spot, flight_adapter_ids, row_adapter_slot, lengths, queries, key_value_cache,
):
    dma = pltpu.SemaphoreType.DMA
    loads = [
        ((ROWS, STEPS, WIDTH), BF16), ((WIDTH,), BF16), ((WIDTH, 1024), BF16), ((WIDTH, 1024), BF16),
        ((64, RANK, WIDTH), BF16), ((64, RANK, HALF), BF16), ((16, 128), jnp.int32), ((1, 64), jnp.int32),
        ((1, ROWS), jnp.int32), ((1, ROWS), jnp.int32), ((ROWS, STEPS, WIDTH), BF16), ((ROWS, SLOTS, 128), BF16),
    ]
    work = [
        ((TOKENS, WIDTH), F32),
        ((QROWS, 128), F32),
        ((QROWS, 128), BF16),
        ((QROWS, 128), BF16),
        ((NR, 4 * TOKENS + 16, 128), BF16),
        ((NF, BLOCK, WIDTH + 128), BF16),
        ((Z, TOKENS + 8, 256), F32),
        ((Z, TOKENS + 8, 256), F32),
        ((TOKENS + 8, 256), F32),
        ((TOKENS + 8, 256), F32),
        ((ROWS, STEPS, WIDTH), BF16),
        ((QROWS, SLOTS), F32),
        ((QROWS, SLOTS), BF16),
        ((QROWS, SLOTS), BF16),
        ((QROWS, 128), F32),
        ((RANK, MET), BF16),
        ((15, RANK, MET), BF16),
        ((NR, 16, 128), BF16),
        ((NR, 16, 128), BF16),
    ]
    sems = [12, NR, NR, NF, NF, Z, Z, 1, 1, 1, 1, 4, 4, 15, 15, NR, NR]
    any_spec = pl.BlockSpec(memory_space=pl.ANY)
    vmem_spec = pl.BlockSpec(memory_space=pltpu.VMEM)
    context, newest = pl.pallas_call(
        body,
        out_shape=(
            jax.ShapeDtypeStruct((ROWS, STEPS, WIDTH), BF16),
            jax.ShapeDtypeStruct((ROWS, STEPS, 128), BF16),
        ),
        in_specs=[any_spec] * 12,
        out_specs=(vmem_spec, vmem_spec),
        scratch_shapes=[pltpu.VMEM(*s) for s in loads + work] + [dma((n,)) for n in sems],
        compiler_params=pltpu.CompilerParams(
            collective_id=0, has_side_effects=True, vmem_limit_bytes=40 * 2**20
        ),
    )(*(pltpu.with_memory_space_constraint(a, pltpu.HBM) for a in (
        layer_input,
        input_norm_gain,
        key_matrix,
        value_matrix,
        adapter_down_factors,
        adapter_up_factors,
        adapter_storage_spot.reshape(16, 128),
        flight_adapter_ids.reshape(1, 64),
        row_adapter_slot.reshape(1, ROWS),
        lengths.reshape(1, ROWS),
        queries.reshape(ROWS, STEPS, WIDTH),
        key_value_cache.reshape(ROWS, SLOTS, 128),
    )))
    context, newest = pl.pallas_call(
        place,
        out_shape=(
            pltpu.HBM((ROWS, STEPS, WIDTH), BF16),
            pltpu.HBM((ROWS, STEPS, 128), BF16),
        ),
        in_specs=[any_spec, any_spec],
        out_specs=(any_spec, any_spec),
        scratch_shapes=[dma((2,))],
    )(pltpu.with_memory_space_constraint(context, pltpu.VMEM), pltpu.with_memory_space_constraint(newest, pltpu.VMEM))
    return context.reshape(ROWS, STEPS, 1, WIDTH), newest.reshape(ROWS, STEPS, 1, 128)


def solution(mesh):
    return jax.shard_map(
        shards,
        mesh=mesh,
        in_specs=(
            P("dp", None, "mp"),
            P("mp"),
            P("mp", None),
            P("mp", None),
            P("dp", None, "mp"),
            P("dp", None, "mp"),
            P(),
            P(),
            P("dp", None),
            P("dp"),
            P("dp", None, "mp", None),
            P("dp", "mp", None, None),
        ),
        out_specs=(P("dp", None, "mp", None), P("dp", None, "mp", None)),
        check_vma=False,
    )
```

```python
import math

import jax
import jax.numpy as jnp
from jax import lax
from jax.experimental import pallas as pl
from jax.experimental.pallas import tpu as pltpu
from jax.sharding import PartitionSpec as P

MESH = pl.DeviceIdType.MESH
F32 = jnp.float32
BF16 = jnp.bfloat16

NORM_EPSILON = 1e-05
ROPE_LOG_BASE = math.log(500000.0)
MASKED_SCORE = -1e30

Y, Z = 8, 8
ROWS, STEPS, CAP, RANK = 16, 2, 4, 16
TOKENS = ROWS * STEPS
GROUPS, HALF, WIDTH, SLOTS = 8, 64, 512, 384
QROWS = TOKENS * GROUPS
BLOCK = CAP * RANK

ROW_OFFS = [(k, 0, 0) for k in (0, 4, 3, 5, 2, 6, 1, 7)]
FAC_OFFS = [(0, a, b) for a in range(2) for b in range(2)]
MP_OFFS = sorted(
    [(a, b) for a in range(2) for b in range(Z) if a or b], key=lambda o: -2 * o[0] - min(o[1], Z - o[1])
)
Z_OFFS = (4, 3, 5, 2, 6, 1, 7)
NR, NF = len(ROW_OFFS), len(FAC_OFFS)
MET = NR * TOKENS

NN = (((1,), (0,)), ((), ()))
NT = (((1,), (1,)), ((), ()))
TN = (((0,), (0,)), ((), ()))


def dot(a, b, dims):
    return lax.dot_general(a, b, dims, preferred_element_type=F32)


def iota(shape, axis):
    return lax.broadcasted_iota(jnp.int32, shape, axis)


CODE_RATE, CODE_SHIFT = 1.75, 124.0


def encode(score):
    power = jnp.exp2(jnp.abs(score) * CODE_RATE - CODE_SHIFT)
    return jnp.where(score < 0.0, -power, power).astype(BF16)


def decode(code):
    power = code.astype(F32)
    size = (jnp.log2(jnp.abs(power)) + CODE_SHIFT) * (1.0 / CODE_RATE)
    return jnp.where(power < 0.0, -size, size)


def body(
    x_hbm, gain_hbm, k_hbm, v_hbm, down_hbm, up_hbm, spot_hbm, ids_hbm, slot_hbm, len_hbm, q_hbm, cache_hbm,
    ctx_ref, new_ref,
    x_v, gain_v, k_v, v_v, down_v, up_v, spot_v, ids_v, slot_v, len_v, q_v, cache_v,
    flat, qexp, qown, qfull, rows, facs, zsend, zrecv, xsend, xrecv, qother,
    own, coded, other, ctxs, mps, mprecv, rets, retrecv,
    load_sem, rows_s, rows_r, facs_s, facs_r, z_s, z_r, x_s, x_r, q_s, q_r, sc_s, sc_r,
    mp_s, mp_r, ret_s, ret_r,
):
    dp, mp = lax.axis_index("dp"), lax.axis_index("mp")
    x_lo, y, core = dp // (2 * Y), (dp // 2) % Y, dp % 2
    half, z = mp // Z, mp % Z

    def along_dp(off, sign):
        to_y = (y + (Y + sign * off[0])) % Y
        return (((x_lo + off[1]) % 2) * (2 * Y) + to_y * 2 + (core + off[2]) % 2, mp)

    def along_mp(off):
        return (dp, ((half + off[0]) % 2) * Z + (z + off[1]) % Z)

    partner = (dp, (1 - half) * Z + z)

    barrier = pltpu.get_barrier_semaphore()
    greeted = [along_dp(o, 1) for o in ROW_OFFS + FAC_OFFS if o != (0, 0, 0)]
    greeted += [along_mp(o) for o in MP_OFFS]
    for device in greeted:
        pl.semaphore_signal(barrier, inc=1, device_id=device, device_id_type=MESH)

    def load(src, dst, n):
        copy = pltpu.make_async_copy(src, dst, load_sem.at[n])
        copy.start()
        return copy

    small = [
        load(x_hbm, x_v, 0), load(gain_hbm, gain_v, 1), load(spot_hbm, spot_v, 2), load(ids_hbm, ids_v, 3),
        load(slot_hbm, slot_v, 4), load(len_hbm, len_v, 5), load(q_hbm, q_v, 6),
    ]
    load_down, load_up = load(down_hbm, down_v, 7), load(up_hbm, up_v, 8)
    load_k, load_v = load(k_hbm, k_v, 9), load(v_hbm, v_v, 10)
    load_cache = load(cache_hbm, cache_v, 11)

    def send(src, dst, ss, rs, device):
        copy = pltpu.make_async_remote_copy(
            src_ref=src, dst_ref=dst, send_sem=ss, recv_sem=rs, device_id=device, device_id_type=MESH
        )
        copy.start()
        return copy

    for copy in small:
        copy.wait()

    for r in range(ROWS):
        flat[pl.ds(2 * r, 2), :] = x_v[r].astype(F32)
    hidden = flat[0:TOKENS, :]
    gained = (hidden * gain_v[...].astype(F32).reshape(1, WIDTH)).astype(BF16)
    for j in range(4):
        rows[0, TOKENS * j : TOKENS * j + TOKENS, :] = gained[:, 128 * j : 128 * j + 128]
    square = jnp.sum(hidden * hidden, axis=1, keepdims=True)
    lane_t, sub_t = iota((TOKENS, 128), 1), iota((TOKENS, 128), 0)
    diagonal = lane_t == sub_t
    square_row = jnp.sum(jnp.where(diagonal, square, 0.0), axis=0, keepdims=True)

    sub16, lane16 = iota((ROWS, 128), 0), iota((ROWS, 128), 1)
    slot_wide = jnp.pad(slot_v[...].astype(F32), ((0, 0), (0, 128 - ROWS)))
    slot_col = jnp.sum(jnp.where(sub16 == lane16, slot_wide, 0.0), axis=1, keepdims=True)
    tag_row = jnp.sum(
        jnp.where(sub16 == (lane16 % TOKENS) // STEPS, slot_col, 0.0), axis=0, keepdims=True
    )
    rows[0, 4 * TOKENS : 4 * TOKENS + 16, :] = jnp.broadcast_to(tag_row, (16, 128)).astype(BF16)

    pl.semaphore_wait(barrier, len(greeted))

    row_copies = [
        send(rows.at[0], rows.at[k], rows_s.at[k], rows_r.at[k], along_dp(ROW_OFFS[k], 1)) for k in range(1, NR)
    ]
    sub64, lane64 = iota((64, 64), 0), iota((64, 64), 1)
    ids_col = jnp.sum(jnp.where(sub64 == lane64, ids_v[...].astype(F32), 0.0), axis=1, keepdims=True)
    spots = spot_v[...].astype(F32)
    lane_n = iota((64, 128), 1).astype(F32)
    found = jnp.zeros((64, 128), F32)
    for i in range(16):
        found = found + jnp.where(ids_col - (128.0 * i) == lane_n, spots[i : i + 1, :], 0.0)
    place_col = jnp.sum(found, axis=1, keepdims=True)
    place_row = jnp.sum(jnp.where(sub64 == lane64, place_col, 0.0), axis=0, keepdims=True)
    group = dp.astype(F32)
    owner_row = jnp.floor(place_row * (1.0 / 64))
    mine_row = jnp.where(owner_row == group, 1.0, 0.0)
    mine_col = jnp.where(jnp.floor(place_col * (1.0 / 64)) == group, 1.0, 0.0)
    order_row = jnp.sum(jnp.where(sub64 < lane64, mine_col, 0.0), axis=0, keepdims=True)
    sub_f = (sub64 // RANK).astype(F32)
    picks = jnp.where(order_row == sub_f, mine_row, 0.0)
    target = jnp.sum(picks * (place_row - 64.0 * owner_row), axis=1, keepdims=True) * RANK
    target = target + (iota((64, 1), 0) % RANK).astype(F32)
    tag_col = jnp.sum(picks * (lane64 + 1).astype(F32), axis=1, keepdims=True) - 1.0
    select = jnp.where(target == iota((64, 1024), 1).astype(F32), 1.0, 0.0).astype(BF16)

    load_down.wait()
    facs[0, :, 0:WIDTH] = dot(select, down_v[...].reshape(64 * RANK, WIDTH), NN).astype(BF16)
    load_up.wait()
    up_own = dot(select, up_v[...].reshape(64 * RANK, HALF), NN).astype(BF16)
    shift = jnp.where(iota((HALF, 128), 1) == iota((HALF, 128), 0) + HALF, 1.0, 0.0).astype(BF16)
    up_wide = dot(up_own, shift, NN)
    facs[0, :, WIDTH : WIDTH + 128] = jnp.where(iota((64, 128), 1) < HALF, tag_col, up_wide).astype(BF16)

    fac_copies = [
        send(facs.at[0], facs.at[k], facs_s.at[k], facs_r.at[k], along_dp(FAC_OFFS[k], 1)) for k in range(1, NF)
    ]
    q_copy = send(q_v, qother, q_s.at[0], q_r.at[0], partner)

    low = lane_t < HALF
    square_rows = jnp.broadcast_to(square_row, (8, 128))
    for w, (copy, weight) in enumerate(((load_k, k_v), (load_v, v_v))):
        copy.wait()
        part = dot(gained, weight[...], NN)
        here = slice(w * 128, w * 128 + 128)
        for j in range(4):
            first = part[:, j * 128 : j * 128 + 128]
            second = part[:, 512 + j * 128 : 512 + j * 128 + 128]
            zsend[2 * j, 0:TOKENS, here] = jnp.where(low, first, pltpu.roll(second, HALF, 1))
            zsend[2 * j + 1, 0:TOKENS, here] = jnp.where(low, pltpu.roll(first, HALF, 1), second)
        for j in range(Z):
            zsend[j, TOKENS : TOKENS + 8, here] = square_rows
    z_copies = [
        send(zsend.at[(z + k) % Z], zrecv.at[k], z_s.at[k], z_r.at[k], along_mp((0, k))) for k in Z_OFFS
    ]

    def expand(ref):
        for r in range(ROWS):
            flat[pl.ds(2 * r, 2), :] = ref[r].astype(F32)
        for g in range(GROUPS):
            tile = flat[0:TOKENS, (g // 2) * 128 : (g // 2) * 128 + 128]
            if g % 2:
                tile = pltpu.roll(tile, HALF, 1)
            qexp[pl.ds(g, TOKENS, stride=GROUPS), :] = jnp.where(low, tile, 0.0)
        return qexp[0:QROWS, :]

    scale = 1.0 / math.sqrt(2 * HALF)
    own_query = expand(q_v)
    qown[...] = own_query.astype(BF16)
    load_cache.wait()
    for r in range(ROWS):
        here = pl.ds(16 * r, 16)
        piece = dot(qown[here, :], cache_v[r], NT) * scale
        own[here, :] = piece
        coded[here, :] = encode(piece)

    score_copies = []
    for c in range(0, 2):
        here = pl.ds(64 * c, 64)
        score_copies.append(send(coded.at[here], other.at[here], sc_s.at[c], sc_r.at[c], partner))

    for copy in row_copies + fac_copies:
        copy.wait_recv()
    lane_r = iota((16, 128), 1)
    tag_tiles = []
    for j in range((NR + 3) // 4):
        tile = jnp.zeros((16, 128), F32)
        for k in range(4 * j, min(4 * j + 4, NR)):
            tile = jnp.where(lane_r // TOKENS == k % 4, rows[k, 4 * TOKENS : 4 * TOKENS + 16, :].astype(F32), tile)
        tag_tiles.append(tile)
    tag_all = jnp.concatenate(tag_tiles, axis=1)[0:1, :MET]
    fac_tag = facs[:, :, WIDTH : WIDTH + 128].reshape(NF * BLOCK, 128)[:, 0:1].astype(F32)
    same = fac_tag == tag_all
    features = jnp.concatenate(
        [rows[:, TOKENS * j : TOKENS * j + TOKENS, :].reshape(MET, 128) for j in range(4)], axis=1
    )
    met = dot(facs[:, :, 0:WIDTH].reshape(NF * BLOCK, WIDTH), features, NT)
    rank_part = jnp.sum(jnp.where(same, met, 0.0).reshape(NF * CAP, RANK, MET), axis=0)
    mps[...] = rank_part.astype(BF16)
    mp_copies = [
        send(mps, mprecv.at[k], mp_s.at[k], mp_r.at[k], along_mp(o)) for k, o in enumerate(MP_OFFS)
    ]

    for c in range(2, 4):
        here = pl.ds(64 * c, 64)
        score_copies.append(send(coded.at[here], other.at[here], sc_s.at[c], sc_r.at[c], partner))

    for copy in z_copies:
        copy.wait_recv()
    total = zsend[z]
    for k in range(1, Z):
        total = total + zrecv[k]
    xsend[...] = total
    x_copy = send(xsend, xrecv, x_s.at[0], x_r.at[0], partner)

    q_copy.wait_recv()
    other_query = expand(qother)
    upper = half == 1
    first = jnp.where(upper, other_query, own_query)
    second = jnp.where(upper, own_query, other_query)
    qfull[...] = (first + pltpu.roll(second, HALF, 1)).astype(BF16)

    for copy in mp_copies:
        copy.wait_recv()
    rank = rank_part
    for k in range(15):
        rank = rank + mprecv[k].astype(F32)
    spread = jnp.broadcast_to(rank[None], (NF * CAP, RANK, MET)).reshape(NF * BLOCK, MET)
    spread = jnp.where(same, spread, 0.0)
    up_all = facs[:, :, WIDTH : WIDTH + 128].reshape(NF * BLOCK, 128)
    coarse = spread.astype(BF16)
    rest = (spread - coarse.astype(F32)).astype(BF16)
    delta = (dot(coarse, up_all, TN) + dot(rest, up_all, TN)).reshape(NR, TOKENS, 128)
    low_m = iota((NR * 16, 128), 1) < HALF
    rets[...] = jnp.where(
        low_m, pltpu.roll(delta[:, 16:32].reshape(NR * 16, 128), HALF, 1), delta[:, 0:16].reshape(NR * 16, 128)
    ).reshape(NR, 16, 128).astype(BF16)
    ret_copies = [
        send(rets.at[k], retrecv.at[k], ret_s.at[k], ret_r.at[k], along_dp(ROW_OFFS[k], -1))
        for k in range(1, NR)
    ]
    len_wide = jnp.pad(len_v[...].astype(F32), ((0, 0), (0, 128 - ROWS)))
    len_col = jnp.sum(
        jnp.where(iota((QROWS, 128), 1) == iota((QROWS, 128), 0) // 16, len_wide, 0.0), axis=1, keepdims=True
    )
    cache_tops, cache_sums = [], []
    for c in range(4):
        score_copies[c].wait_recv()
        here = pl.ds(64 * c, 64)
        scores = own[here, :] + decode(other[here, :])
        valid = iota((64, SLOTS), 1).astype(F32) < len_col[64 * c : 64 * c + 64]
        scores = jnp.where(valid, scores, MASKED_SCORE)
        top = jnp.max(scores, axis=1, keepdims=True)
        spread = jnp.exp(scores - top)
        cache_tops.append(top)
        cache_sums.append(jnp.sum(spread, axis=1, keepdims=True))
        spread = spread.astype(BF16)
        for r in range(4):
            ctxs[pl.ds(64 * c + 16 * r, 16), :] = dot(spread[16 * r : 16 * r + 16], cache_v[4 * c + r], NN)
    cache_top = jnp.concatenate(cache_tops, axis=0)
    cache_sum = jnp.concatenate(cache_sums, axis=0)

    x_copy.wait_recv()
    total = xsend[...] + xrecv[...]
    squares = jnp.sum(jnp.where(diagonal, total[TOKENS : TOKENS + 1, 0:128], 0.0), axis=1, keepdims=True)
    norm = lax.rsqrt(squares * (1.0 / (16 * WIDTH)) + NORM_EPSILON)
    key_lin = total[0:TOKENS, 0:128] * norm
    pair = (lane_t // 2).astype(F32)
    frequency = jnp.exp(-(2.0 * pair / (2 * HALF)) * ROPE_LOG_BASE)
    start = jnp.sum(jnp.where(lane_t == sub_t // STEPS, len_wide, 0.0), axis=1, keepdims=True)
    angle = (start + (sub_t % STEPS).astype(F32)) * frequency
    even = lane_t % 2 == 0
    turned = jnp.where(even, -pltpu.roll(key_lin, 127, 1), pltpu.roll(key_lin, 1, 1))
    key_rot = key_lin * jnp.cos(angle) + turned * jnp.sin(angle)
    new_key = key_rot.astype(BF16)
    fresh = dot(qfull[...], new_key, NT) * scale
    q_sub, t_lane = iota((QROWS, TOKENS), 0), iota((QROWS, TOKENS), 1)
    counts = (t_lane // STEPS == q_sub // 16) & (t_lane % STEPS <= (q_sub // GROUPS) % STEPS)
    fresh = jnp.where(counts, fresh, MASKED_SCORE)
    top = jnp.maximum(cache_top, jnp.max(fresh, axis=1, keepdims=True))
    fresh_exp = jnp.exp(fresh - top)
    shrink = jnp.exp(cache_top - top)
    inverse = 1.0 / (cache_sum * shrink + jnp.sum(fresh_exp, axis=1, keepdims=True))
    fresh_weights = (fresh_exp * inverse).astype(BF16)
    ctxs[...] = ctxs[...] * (shrink * inverse)
    key_own = jnp.where(upper, pltpu.roll(key_rot, HALF, 1), key_rot)
    value_base = total[0:TOKENS, 128:256]
    value_base = jnp.where(upper, value_base, pltpu.roll(value_base, HALF, 1))

    lora = rets[0].astype(F32)
    for copy in ret_copies:
        copy.wait_recv()
    for k in range(1, NR):
        lora = lora + retrecv[k].astype(F32)
    lora = jnp.concatenate([lora, pltpu.roll(lora, HALF, 1)], axis=0)

    new_value = ((value_base + 2.0 * lora) * norm).astype(BF16)
    flat[0:TOKENS, 0:128] = jnp.where(low, key_own, (value_base + 2.0 * lora) * norm)
    for r in range(ROWS):
        new_ref[r] = flat[pl.ds(2 * r, 2), 0:128].astype(BF16)
    qexp[0:QROWS, :] = ctxs[...] + dot(fresh_weights, new_value, NN)
    for j in range(4):
        left = qexp[pl.ds(2 * j, TOKENS, stride=GROUPS), :]
        right = qexp[pl.ds(2 * j + 1, TOKENS, stride=GROUPS), :]
        flat[0:TOKENS, j * 128 : j * 128 + 128] = jnp.where(low, pltpu.roll(left, HALF, 1), right)
    for r in range(ROWS):
        ctx_ref[r] = flat[pl.ds(2 * r, 2), :].astype(BF16)

    for copy in (
        row_copies + fac_copies + z_copies + score_copies + mp_copies + ret_copies + [q_copy, x_copy]
    ):
        copy.wait_send()


def place(ctx_ref, new_ref, ctx_out, new_out, sem):
    first = pltpu.make_async_copy(ctx_ref, ctx_out, sem.at[0])
    second = pltpu.make_async_copy(new_ref, new_out, sem.at[1])
    first.start()
    second.start()
    first.wait()
    second.wait()


def shards(
    layer_input, input_norm_gain, key_matrix, value_matrix, adapter_down_factors, adapter_up_factors,
    adapter_storage_spot, flight_adapter_ids, row_adapter_slot, lengths, queries, key_value_cache,
):
    dma = pltpu.SemaphoreType.DMA
    loads = [
        ((ROWS, STEPS, WIDTH), BF16), ((WIDTH,), BF16), ((WIDTH, 1024), BF16), ((WIDTH, 1024), BF16),
        ((64, RANK, WIDTH), BF16), ((64, RANK, HALF), BF16), ((16, 128), jnp.int32), ((1, 64), jnp.int32),
        ((1, ROWS), jnp.int32), ((1, ROWS), jnp.int32), ((ROWS, STEPS, WIDTH), BF16), ((ROWS, SLOTS, 128), BF16),
    ]
    work = [
        ((TOKENS + 8, WIDTH), F32),
        ((QROWS + 8, 128), F32),
        ((QROWS, 128), BF16),
        ((QROWS, 128), BF16),
        ((NR, 4 * TOKENS + 16, 128), BF16),
        ((NF, BLOCK, WIDTH + 128), BF16),
        ((Z, TOKENS + 8, 256), F32),
        ((Z, TOKENS + 8, 256), F32),
        ((TOKENS + 8, 256), F32),
        ((TOKENS + 8, 256), F32),
        ((ROWS, STEPS, WIDTH), BF16),
        ((QROWS, SLOTS), F32),
        ((QROWS, SLOTS), BF16),
        ((QROWS, SLOTS), BF16),
        ((QROWS, 128), F32),
        ((RANK, MET), BF16),
        ((15, RANK, MET), BF16),
        ((NR, 16, 128), BF16),
        ((NR, 16, 128), BF16),
    ]
    sems = [12, NR, NR, NF, NF, Z, Z, 1, 1, 1, 1, 4, 4, 15, 15, NR, NR]
    any_spec = pl.BlockSpec(memory_space=pl.ANY)
    vmem_spec = pl.BlockSpec(memory_space=pltpu.VMEM)
    context, newest = pl.pallas_call(
        body,
        out_shape=(
            jax.ShapeDtypeStruct((ROWS, STEPS, WIDTH), BF16),
            jax.ShapeDtypeStruct((ROWS, STEPS, 128), BF16),
        ),
        in_specs=[any_spec] * 12,
        out_specs=(vmem_spec, vmem_spec),
        scratch_shapes=[pltpu.VMEM(*s) for s in loads + work] + [dma((n,)) for n in sems],
        compiler_params=pltpu.CompilerParams(
            collective_id=0, has_side_effects=True, vmem_limit_bytes=40 * 2**20
        ),
    )(*(pltpu.with_memory_space_constraint(a, pltpu.HBM) for a in (
        layer_input,
        input_norm_gain,
        key_matrix,
        value_matrix,
        adapter_down_factors,
        adapter_up_factors,
        adapter_storage_spot.reshape(16, 128),
        flight_adapter_ids.reshape(1, 64),
        row_adapter_slot.reshape(1, ROWS),
        lengths.reshape(1, ROWS),
        queries.reshape(ROWS, STEPS, WIDTH),
        key_value_cache.reshape(ROWS, SLOTS, 128),
    )))
    context, newest = pl.pallas_call(
        place,
        out_shape=(
            pltpu.HBM((ROWS, STEPS, WIDTH), BF16),
            pltpu.HBM((ROWS, STEPS, 128), BF16),
        ),
        in_specs=[any_spec, any_spec],
        out_specs=(any_spec, any_spec),
        scratch_shapes=[dma((2,))],
    )(pltpu.with_memory_space_constraint(context, pltpu.VMEM), pltpu.with_memory_space_constraint(newest, pltpu.VMEM))
    return context.reshape(ROWS, STEPS, 1, WIDTH), newest.reshape(ROWS, STEPS, 1, 128)


def solution(mesh):
    return jax.shard_map(
        shards,
        mesh=mesh,
        in_specs=(
            P("dp", None, "mp"),
            P("mp"),
            P("mp", None),
            P("mp", None),
            P("dp", None, "mp"),
            P("dp", None, "mp"),
            P(),
            P(),
            P("dp", None),
            P("dp"),
            P("dp", None, "mp", None),
            P("dp", "mp", None, None),
        ),
        out_specs=(P("dp", None, "mp", None), P("dp", None, "mp", None)),
        check_vma=False,
    )
```
